256 devices in a mesh: rep: 8 (over y, core), wide: 32 (over z, x).
Axes of the slice: x: 4, y: 4, z: 8, core: 2. Of those that a mesh axis runs over, the one named last changes fastest.
Arguments:
- shard_lost: int32 [8], replicated, may hold values from 0 to 31, as said below
- new_blocks: int32 [28], replicated, may hold values from 1 to 3, as said below
- weights: float32 [8, 4096, 1536], P('rep', 'wide'), may hold values from -3 to 3, as said below
- first_moment: float32 [8, 4096, 1536], P('rep', 'wide'), may hold values from -2 to 2, as said below
- second_moment: float32 [8, 4096, 1536], P('rep', 'wide'), may hold values from 0.05 to 1, as said below
- gradient: bfloat16 [8, 4096, 1536], P('rep', 'wide'), may hold values from -1200 to 1200
Outputs:
- new_weights: float32 [8, 12288, 1536], P('rep', 'wide')
- new_first: float32 [8, 12288, 1536], P('rep', 'wide')
- new_second: float32 [8, 12288, 1536], P('rep', 'wide')
The draws below stay inside these ranges and needn't reach their ends.
Inputs may be any that keep to these rules, and one draw needn't show every extreme that they name: `shard_lost`: the 8 values are distinct; one island lost shard 0 and another lost the last shard. `new_blocks`: the counts sum to 32; exactly one of them equals 3. All islands hold the same weights, except the 128 rows that each island lost at its lost shard, which hold arbitrary values. `first_moment`: same for the first moments. `second_moment`: same for the second moments.
All inputs are finite; a program needn't handle non-finite values.
Results may differ from the reference program's by a relative error of at most 0.0003.
Values may be sent and summed in bfloat16 or wider, within the bound.
A program may use at most 64 MiB of HBM per device.

```python
import math
import jax
import jax.numpy as jnp
from jax import lax

FF = 1536
BLOCK = 128
ISLANDS = 8
OLD_SHARDS = 32
NEW_SHARDS = 28
CAP_BLK = 3
CAP_ROWS = 384
ROWS = 4096
N_WIDE = 32


def failure(key):
    base = jax.random.fold_in(key, 9001)
    middle = 1 + jax.random.permutation(jax.random.fold_in(base, 2), OLD_SHARDS - 2)
    ends = jnp.array([0, OLD_SHARDS - 1], jnp.int32)
    chosen = jnp.concatenate([ends, middle[:ISLANDS - 2].astype(jnp.int32)])
    placing = jax.random.permutation(jax.random.fold_in(base, 3), ISLANDS)
    return chosen[placing].astype(jnp.int32)


def draw_shard_lost(key, part):
    return failure(key)


def draw_new_blocks(key, part):
    extra = OLD_SHARDS - NEW_SHARDS
    biggest = CAP_BLK - 1
    others = extra - biggest
    added = jnp.zeros((NEW_SHARDS,), jnp.int32)
    if others >= 1:
        order = 1 + jax.random.permutation(jax.random.fold_in(key, 313), NEW_SHARDS - 1)
        added = added.at[0].set(1)
        added = added.at[order[0]].set(biggest)
        added = added.at[order[1:others]].set(1)
    else:
        order = jax.random.permutation(jax.random.fold_in(key, 313), NEW_SHARDS)
        added = added.at[order[0]].set(biggest)
    return (1 + added).astype(jnp.int32)


def replicated(key, common, broken):
    shards = failure(key)
    whole = jnp.broadcast_to(common[None], (ISLANDS, ROWS, FF))
    for island in range(ISLANDS):
        whole = lax.dynamic_update_slice(whole, broken[island][None], (jnp.int32(island), shards[island] * BLOCK, jnp.int32(0)))
    return whole


def draw_weights(key, part):
    first_key = jax.random.fold_in(key, 11)
    second_key = jax.random.fold_in(key, 12)
    common = jnp.clip(0.5 * jax.random.normal(first_key, (ROWS, FF), jnp.float32), -3.0, 3.0)
    broken = jax.random.uniform(second_key, (ISLANDS, BLOCK, FF), jnp.float32, -3.0, 3.0)
    return replicated(key, common, broken).astype(jnp.float32)


def draw_first_moment(key, part):
    first_key = jax.random.fold_in(key, 21)
    second_key = jax.random.fold_in(key, 22)
    common = jnp.clip(0.3 * jax.random.normal(first_key, (ROWS, FF), jnp.float32), -2.0, 2.0)
    broken = jax.random.uniform(second_key, (ISLANDS, BLOCK, FF), jnp.float32, -2.0, 2.0)
    return replicated(key, common, broken).astype(jnp.float32)


def draw_second_moment(key, part):
    first_key = jax.random.fold_in(key, 31)
    second_key = jax.random.fold_in(key, 32)
    common = jnp.exp(jax.random.uniform(first_key, (ROWS, FF), jnp.float32, math.log(0.05), 0.0))
    broken = jnp.exp(jax.random.uniform(second_key, (ISLANDS, BLOCK, FF), jnp.float32, math.log(0.05), 0.0))
    return replicated(key, common, broken).astype(jnp.float32)


def draw_gradient(key, part):
    noise_key = jax.random.fold_in(key, 41)
    row_key = jax.random.fold_in(key, 42)
    col_key = jax.random.fold_in(key, 43)
    pick_key = jax.random.fold_in(key, 45)
    ramp = jnp.power(3.0, jnp.arange(ROWS, dtype=jnp.float32) / ROWS)[None, :, None]
    ranked = jax.random.permutation(pick_key, ISLANDS)
    quiet_islands = ranked < max(1, ISLANDS // 4)
    noise = jnp.clip(jax.random.normal(noise_key, (ISLANDS, ROWS, FF), jnp.float32), -4.0, 4.0)
    rows_scale = jnp.exp(jax.random.uniform(row_key, (ISLANDS, ROWS, 1), jnp.float32, 0.0, math.log(10.0)))
    island_scale = jnp.where(quiet_islands, 1.0 / 250.0, 1.0)
    cols_scale = jnp.exp(jax.random.uniform(col_key, (1, 1, FF), jnp.float32, 0.0, math.log(10.0)))
    scaled = noise * rows_scale * cols_scale * ramp * island_scale.astype(jnp.float32)[:, None, None]
    return scaled.astype(jnp.bfloat16)


def setup_inputs(seed: int = 0) -> dict:
    key_of = jax.random.split(jax.random.key(seed), 7)
    shard_lost = draw_shard_lost(jax.random.fold_in(key_of[6], 71), 0)
    new_blocks = draw_new_blocks(jax.random.fold_in(key_of[6], 71), 0)
    weights = draw_weights(jax.random.fold_in(key_of[6], 71), 0)
    first_moment = draw_first_moment(jax.random.fold_in(key_of[6], 71), 0)
    second_moment = draw_second_moment(jax.random.fold_in(key_of[6], 71), 0)
    gradient = draw_gradient(jax.random.fold_in(key_of[6], 71), 0)
    return {"shard_lost": shard_lost, "new_blocks": new_blocks, "weights": weights, "first_moment": first_moment, "second_moment": second_moment, "gradient": gradient}


beta_first = 0.9
beta_second = 0.95
bias_first = 1.0 - 0.9 ** 20
bias_second = 1.0 - 0.95 ** 20
learn_rate = 0.01
weight_decay = 0.1
eps_adam = 1e-08

def adam_update(params, moment_one, moment_two, grad_in, factor):
    clipped = grad_in.astype(jnp.float32) * factor
    one_new = beta_first * moment_one + (1.0 - beta_first) * clipped
    two_new = beta_second * moment_two + (1.0 - beta_second) * clipped * clipped
    step_dir = one_new / bias_first / (jnp.sqrt(two_new / bias_second) + eps_adam)
    params_new = params - learn_rate * (step_dir + weight_decay * params)
    return (params_new, one_new, two_new)

def reference(shard_lost, new_blocks, weights, first_moment, second_moment, gradient):

    def recover(array):
        pieces = []
        for island in range(ISLANDS):
            lost_row = (shard_lost[island] * BLOCK).astype(jnp.int32)
            healthy = array[(island + 1) % ISLANDS]
            pieces.append(lax.dynamic_slice_in_dim(healthy, lost_row, BLOCK, 0))
        result = array
        for island in range(ISLANDS):
            lost_row = (shard_lost[island] * BLOCK).astype(jnp.int32)
            result = lax.dynamic_update_slice(result, pieces[island][None], (jnp.int32(island), lost_row, jnp.int32(0)))
        return result
    counts = jnp.concatenate([new_blocks, jnp.zeros((N_WIDE // 8,), jnp.int32)])
    starts = jnp.cumsum(counts) - counts
    slots = jnp.arange(N_WIDE * CAP_ROWS, dtype=jnp.int32)
    owner = slots // CAP_ROWS
    within = slots % CAP_ROWS
    valid = within < counts[owner] * BLOCK
    source_rows = jnp.minimum(starts[owner] * BLOCK + within, ROWS - 1).astype(jnp.int32)
    limit = 0.5 * math.sqrt(ROWS * FF)

    def per_island(items):
        params, moment_one, moment_two, grad_in = items
        norm_sum = jnp.sum(jnp.square(grad_in.astype(jnp.float32)))
        factor = jnp.minimum(1.0, limit / (jnp.sqrt(norm_sum) + 1e-06))
        updated = adam_update(params, moment_one, moment_two, grad_in, factor)
        return tuple((jnp.where(valid[:, None], jnp.take(item, source_rows, axis=0), 0.0) for item in updated))
    outputs = lax.map(per_island, (recover(weights), recover(first_moment), recover(second_moment), gradient))
    return (outputs[0], outputs[1], outputs[2])
```

```python
import functools
import math

import jax
import jax.numpy as jnp
from jax import lax
from jax.experimental import pallas as pl
from jax.experimental.pallas import tpu as pltpu
from jax.sharding import PartitionSpec as P

beta_first = 0.9
beta_second = 0.95
bias_first = 1.0 - 0.9**20
bias_second = 1.0 - 0.95**20
learn_rate = 0.01
weight_decay = 0.1
eps_adam = 1e-08

WIDE = 32
REP = 8
SHIFT = 4
SLOTS = 3
STAGE_TWO = tuple(range(4, WIDE, 4))
MESH = pl.DeviceIdType.MESH


def gather_kernel(
    lost_ref, blocks_ref, w_ref, m_ref, v_ref, g_ref,
    gat_ref, gwin_ref, norm_ref, meta_ref,
    own, fix, win_w, win_m, win_v, sel, gv, part_one, part_two,
    loc, fix_s, fix_r, win_s, win_r, g_s, g_r, one_s, one_r, two_s, two_r, y_s, y_r, c_s, c_r,
):
    arrays = (w_ref, m_ref, v_ref)
    wins = (win_w, win_m, win_v)
    rows = own.shape[1]
    island = lax.axis_index("rep")
    shard = lax.axis_index("wide")
    partner = island + 1 - 2 * lax.rem(island, 2)

    def lower(d):
        return {"rep": island, "wide": lax.rem(shard + WIDE - d, WIDE)}

    def higher(d):
        return {"rep": island, "wide": lax.rem(shard + d, WIDE)}

    def along_y(dy):
        return lax.rem(island + 2 * dy, REP)

    def piece(p):
        return pl.ds(pl.multiple_of(p * rows, rows), rows)

    def remote(src, dst, s, r, where):
        return pltpu.make_async_remote_copy(src, dst, s, r, device_id=where, device_id_type=MESH)

    to_partner = {"rep": partner, "wide": shard}

    own_in = [pltpu.make_async_copy(arrays[a].at[piece(island)], own.at[a], loc.at[a]) for a in range(3)]
    grad_in = pltpu.make_async_copy(g_ref, gv, loc.at[3])
    grad_own = pltpu.make_async_copy(g_ref, gwin_ref.at[0], loc.at[4])
    grad_in.start()
    for copy in own_in:
        copy.start()

    barrier = pltpu.get_barrier_semaphore()
    offsets = (1, 2, 3, *STAGE_TWO)
    for d in offsets:
        pl.semaphore_signal(barrier, inc=1, device_id=higher(d), device_id_type=MESH)
    for dy in range(1, 4):
        pl.semaphore_signal(barrier, inc=1, device_id={"rep": along_y(dy), "wide": shard}, device_id_type=MESH)
    pl.semaphore_signal(barrier, inc=1, device_id=to_partner, device_id_type=MESH)
    pl.semaphore_wait(barrier, len(offsets) + 4)

    mend = [remote(arrays[a].at[piece(partner)], fix.at[a], fix_s.at[a], fix_r.at[a], to_partner) for a in range(3)]
    for copy in mend:
        copy.start()

    grad_in.wait()
    grad_own.start()
    step = 16

    def add_rows(i, total):
        x = gv[pl.ds(pl.multiple_of(i * step, step), step), :].astype(jnp.float32)
        return total + fold(x * x)

    def fold(sq):
        top = sq[:8] + sq[8:]
        parts = [top[:, 128 * c : 128 * (c + 1)] for c in range(top.shape[1] // 128)]
        while len(parts) > 1:
            parts = [sum(parts[i : i + 2][1:], parts[i]) for i in range(0, len(parts), 2)]
        return parts[0]

    part_one[0] = lax.fori_loop(0, gv.shape[0] // step, add_rows, jnp.zeros((8, 128), jnp.float32))
    ones = [remote(part_one.at[0], part_one.at[d], one_s.at[d - 1], one_r.at[d - 1], lower(d)) for d in range(1, 4)]
    for copy in ones:
        copy.start()

    first = jnp.int32(0)
    count = jnp.int32(0)
    for k in range(blocks_ref.shape[0]):
        n = blocks_ref[k]
        first = first + jnp.where(k < shard, n, 0)
        count = count + jnp.where(k == shard, n, 0)
    gaps = [jnp.clip(first + s - shard, 0, SHIFT) for s in range(SLOTS)]
    meta_ref[0] = count
    for s in range(SLOTS):
        meta_ref[1 + s] = gaps[s]
    broken = lost_ref[island] == shard

    windows = []
    for a in range(3):
        own_in[a].wait()
        mend[a].wait_recv()
        wins[a][0] = jnp.where(broken, fix[a], own[a])
        sends = [
            remote(wins[a].at[0], wins[a].at[d], win_s.at[a, d - 1], win_r.at[a, d - 1], lower(d))
            for d in range(1, SHIFT + 1)
        ]
        for copy in sends:
            copy.start()
        windows.append(sends)

    grads = [remote(g_ref, gwin_ref.at[d], g_s.at[d - 1], g_r.at[d - 1], lower(d)) for d in range(1, SHIFT + 1)]
    for copy in grads:
        copy.start()

    for copy in ones:
        copy.wait_recv()
    part_two[0] = part_one[0] + part_one[1] + part_one[2] + part_one[3]
    twos = [
        remote(part_two.at[0], part_two.at[k + 1], two_s.at[k], two_r.at[k], lower(d))
        for k, d in enumerate(STAGE_TWO)
    ]
    for copy in twos:
        copy.start()

    kept, crossed, passed = [], [], []
    for a in range(3):
        for copy in windows[a]:
            copy.wait_recv()
        for s in range(SLOTS):
            sel[a, s] = wins[a][gaps[s]]
        mine = gat_ref.at[a, :, piece(island)]
        keep = pltpu.make_async_copy(sel.at[a], mine, loc.at[5 + a])
        sends = [
            remote(sel.at[a], mine, y_s.at[a, dy - 1], y_r.at[a, dy - 1], {"rep": along_y(dy), "wide": shard})
            for dy in range(1, 4)
        ]
        over = remote(sel.at[a], mine, c_s.at[a, 0], c_r.at[a, 0], to_partner)
        for copy in (*sends, over, keep):
            copy.start()
        kept.append(keep)
        crossed.append(sends)
        passed.append([over])
    for a in range(3):
        for dy in range(1, 4):
            theirs = gat_ref.at[a, :, piece(lax.rem(island + REP - 2 * dy, REP))]
            remote(sel.at[a], theirs, y_s.at[a, dy - 1], y_r.at[a, dy - 1], to_partner).wait_recv()
            over = remote(theirs, theirs, c_s.at[a, dy], c_r.at[a, dy], to_partner)
            over.start()
            passed[a].append(over)

    for copy in twos:
        copy.wait_recv()
    total = part_two[0]
    for k in range(1, len(STAGE_TWO) + 1):
        total = total + part_two[k]
    norm_ref[...] = total

    for copy in (*mend, *ones, *twos):
        copy.wait_send()
    grad_own.wait()
    for copy in grads:
        copy.wait()
    for a in range(3):
        kept[a].wait()
        for copy in (*windows[a], *crossed[a]):
            copy.wait_send()
        for copy in passed[a]:
            copy.wait()


def update_kernel(limit, meta_ref, norm_ref, gat_ref, g_ref, w_out, m_out, v_out, factor_ref):
    slot, part = pl.program_id(0), pl.program_id(1)

    @pl.when(jnp.logical_and(slot == 0, part == 0))
    def _():
        norm_sum = jnp.sum(norm_ref[...], keepdims=True)
        factor_ref[...] = jnp.broadcast_to(jnp.minimum(1.0, limit / (jnp.sqrt(norm_sum) + 1e-06)), factor_ref.shape)

    @pl.when(slot < meta_ref[0])
    def _():
        factor = factor_ref[0:1, 0:1]
        params, moment_one, moment_two = gat_ref[0, 0], gat_ref[1, 0], gat_ref[2, 0]
        clipped = g_ref[0].astype(jnp.float32) * factor
        one_new = beta_first * moment_one + (1.0 - beta_first) * clipped
        two_new = beta_second * moment_two + (1.0 - beta_second) * clipped * clipped
        step_dir = one_new / bias_first / (jnp.sqrt(two_new / bias_second) + eps_adam)
        w_out[...] = params - learn_rate * (step_dir + weight_decay * params)
        m_out[...] = one_new
        v_out[...] = two_new

    @pl.when(slot >= meta_ref[0])
    def _():
        for out in (w_out, m_out, v_out):
            out[...] = jnp.zeros_like(out)


def on_device(shard_lost, new_blocks, weights, first_moment, second_moment, gradient):
    _, block, ff = weights.shape
    rows = block // REP
    f32 = jnp.float32
    vmem, anywhere = pl.BlockSpec(memory_space=pltpu.VMEM), pl.BlockSpec(memory_space=pl.ANY)
    smem = pl.BlockSpec(memory_space=pltpu.SMEM)
    dma = lambda *shape: pltpu.SemaphoreType.DMA(shape)
    gat, gwin, norm, meta = pl.pallas_call(
        gather_kernel,
        out_shape=(
            jax.ShapeDtypeStruct((3, SLOTS, block, ff), f32),
            jax.ShapeDtypeStruct((SHIFT + 1, block, ff), jnp.bfloat16),
            jax.ShapeDtypeStruct((8, 128), f32),
            jax.ShapeDtypeStruct((8,), jnp.int32),
        ),
        in_specs=[smem, smem] + [anywhere] * 4,
        out_specs=(anywhere, anywhere, vmem, smem),
        scratch_shapes=[
            pltpu.VMEM((3, rows, ff), f32),
            pltpu.VMEM((3, rows, ff), f32),
            *[pltpu.VMEM((SHIFT + 1, rows, ff), f32)] * 3,
            pltpu.VMEM((3, SLOTS, rows, ff), f32),
            pltpu.VMEM((block, ff), jnp.bfloat16),
            pltpu.VMEM((4, 8, 128), f32),
            pltpu.VMEM((8, 8, 128), f32),
            dma(8), dma(3), dma(3), dma(3, 4), dma(3, 4), dma(4), dma(4),
            dma(3), dma(3), dma(7), dma(7), dma(3, 3), dma(3, 3), dma(3, 4), dma(3, 4),
        ],
        compiler_params=pltpu.CompilerParams(
            collective_id=0, has_side_effects=True, vmem_limit_bytes=24 * 2**20
        ),
        name="gather_blocks",
    )(shard_lost, new_blocks, weights[0], first_moment[0], second_moment[0], gradient[0])

    chunk = 64
    parts = block // chunk

    def source(slot, part, meta_ref):
        last = jnp.maximum(meta_ref[0], 1) - 1
        return jnp.minimum(slot, last), jnp.where(slot > last, parts - 1, part)

    def gat_map(slot, part, meta_ref):
        s, i = source(slot, part, meta_ref)
        return 0, s, i, 0

    def grad_map(slot, part, meta_ref):
        s, i = source(slot, part, meta_ref)
        return meta_ref[1 + s], i, 0

    out_spec = pl.BlockSpec((chunk, ff), lambda slot, part, meta_ref: (slot * parts + part, 0))
    limit = 0.5 * math.sqrt(block * WIDE * ff)
    outs = pl.pallas_call(
        functools.partial(update_kernel, limit),
        out_shape=[jax.ShapeDtypeStruct((SLOTS * block, ff), f32)] * 3,
        grid_spec=pltpu.PrefetchScalarGridSpec(
            num_scalar_prefetch=1,
            grid=(SLOTS, parts),
            in_specs=[
                pl.BlockSpec((8, 128), lambda slot, part, meta_ref: (0, 0)),
                pl.BlockSpec((3, 1, chunk, ff), gat_map),
                pl.BlockSpec((1, chunk, ff), grad_map),
            ],
            out_specs=[out_spec] * 3,
            scratch_shapes=[pltpu.VMEM((8, 128), f32)],
        ),
        compiler_params=pltpu.CompilerParams(vmem_limit_bytes=24 * 2**20),
        name="adam_update",
    )(meta, norm, gat, gwin)
    return tuple(out[None] for out in outs)


def solution(mesh):
    split = P("rep", "wide", None)
    return jax.shard_map(
        on_device,
        mesh=mesh,
        in_specs=(P(), P(), split, split, split, split),
        out_specs=(split, split, split),
        check_vma=False,
    )
```

```python
import functools
import math

import jax
import jax.numpy as jnp
from jax import lax
from jax.experimental import pallas as pl
from jax.experimental.pallas import tpu as pltpu
from jax.sharding import PartitionSpec as P

beta_first = 0.9
beta_second = 0.95
bias_first = 1.0 - 0.9**20
bias_second = 1.0 - 0.95**20
learn_rate = 0.01
weight_decay = 0.1
eps_adam = 1e-08

WIDE = 32
REP = 8
SHIFT = 4
SLOTS = 3
LANES = 128
TOP = 32767.0
CHUNKS = 4
STAGE_TWO = tuple(range(4, WIDE, 4))
MESH = pl.DeviceIdType.MESH


def encode(x, out):
    size = jnp.abs(x)
    most = jnp.clip(jnp.max(size, axis=1, keepdims=True), 2.0**-120, 2.0**120)
    exponent = jnp.ceil(jnp.log2(most))
    code = jnp.minimum(jnp.round(jnp.sqrt(size * jnp.exp2(-exponent)) * TOP), TOP)
    code = jnp.where(x < 0, -code, code)
    out[:, : x.shape[1]] = code.astype(jnp.int32).astype(jnp.int16)
    tail = jnp.broadcast_to(exponent, (x.shape[0], LANES))
    out[:, x.shape[1] :] = tail.astype(jnp.int32).astype(jnp.int16)


def decode(x):
    columns = x.shape[1] - LANES
    code = x[:, :columns].astype(jnp.int32).astype(jnp.float32)
    scale = jnp.exp2(x[:, columns:].astype(jnp.int32).astype(jnp.float32)) * (1.0 / TOP**2)
    return code * jnp.abs(code) * jnp.concatenate([scale] * (columns // LANES), axis=1)


def fold(squares):
    top = squares[:8] + squares[8:]
    parts = [top[:, LANES * c : LANES * (c + 1)] for c in range(top.shape[1] // LANES)]
    while len(parts) > 1:
        parts = [sum(parts[i : i + 2][1:], parts[i]) for i in range(0, len(parts), 2)]
    return parts[0]


def gather_kernel(
    lost_hbm, blocks_hbm, w_ref, m_ref, v_ref, g_ref,
    gat_ref, gwin_ref, norm_ref, meta_ref,
    lost_ref, blocks_ref, own, fix, win_w, win_m, win_v, sel, gv, part_one, part_two, loc, out_sem, in_sem,
):
    arrays = (w_ref, m_ref, v_ref)
    wins = (win_w, win_m, win_v)
    rows = own.shape[1]
    island = lax.axis_index("rep")
    shard = lax.axis_index("wide")
    partner = island + 1 - 2 * lax.rem(island, 2)
    width = sel.shape[3]
    middle = width // LANES // 2 * LANES
    left, right = pl.ds(0, middle), pl.ds(middle, width - middle)
    to_partner = {"rep": partner, "wide": shard}
    used = {"remote": 0, "local": 0}

    def lower(d):
        return {"rep": island, "wide": lax.rem(shard + WIDE - d, WIDE)}

    def higher(d):
        return {"rep": island, "wide": lax.rem(shard + d, WIDE)}

    def along_y(dy):
        return lax.rem(island + REP + 2 * dy, REP)

    def chip_y(dy):
        return {"rep": along_y(dy), "wide": shard}

    def piece(p):
        return pl.ds(pl.multiple_of(p * rows, rows), rows)

    def send(src, dst, where, lands=None):
        k = used["remote"]
        used["remote"] = k + 1
        copy = pltpu.make_async_remote_copy(src, dst, out_sem.at[k], in_sem.at[k], device_id=where, device_id_type=MESH)
        copy.start()
        if lands is None:
            return copy, copy
        return copy, pltpu.make_async_remote_copy(
            src, lands, out_sem.at[k], in_sem.at[k], device_id=where, device_id_type=MESH
        )

    def local(src, dst):
        k = used["local"]
        used["local"] = k + 1
        copy = pltpu.make_async_copy(src, dst, loc.at[k])
        copy.start()
        return copy

    sent, kept = [], []

    def ship(*args, **kwargs):
        copy, lands = send(*args, **kwargs)
        sent.append(copy)
        return lands

    grad_in = local(g_ref, gv)
    own_in = [local(arrays[a].at[piece(island)], own.at[a]) for a in range(3)]
    lost_in, blocks_in = local(lost_hbm, lost_ref), local(blocks_hbm, blocks_ref)

    barrier = pltpu.get_barrier_semaphore()
    offsets = (1, 2, 3, *STAGE_TWO, WIDE - 1)
    greeted = [*(higher(d) for d in offsets), chip_y(1), chip_y(-1), to_partner]
    for device in greeted:
        pl.semaphore_signal(barrier, inc=1, device_id=device, device_id_type=MESH)
    pl.semaphore_wait(barrier, len(greeted))

    mend = [ship(arrays[a].at[piece(partner)], fix.at[a], to_partner) for a in range(3)]

    gstep = gv.shape[0] // CHUNKS
    gone = [pl.ds(c * gstep, gstep) for c in range(CHUNKS)]
    grad_four, grad_one = [], []

    def send_gradient(c):
        grad_four.append(ship(g_ref.at[gone[c]], gwin_ref.at[4, gone[c]], lower(4)))
        grad_one.append(ship(g_ref.at[gone[c]], gwin_ref.at[1, gone[c]], lower(1)))

    send_gradient(0)

    lost_in.wait()
    blocks_in.wait()
    first = jnp.int32(0)
    count = jnp.int32(0)
    for k in range(blocks_ref.shape[0]):
        n = blocks_ref[k]
        first = first + jnp.where(k < shard, n, 0)
        count = count + jnp.where(k == shard, n, 0)
    gaps = [jnp.clip(first + s - shard, 0, SHIFT) for s in range(SLOTS)]
    meta_ref[0] = count
    for s in range(SLOTS):
        meta_ref[1 + s] = gaps[s]
    broken = lost_ref[island] == shard

    got = []
    for a in range(3):
        own_in[a].wait()
        mend[a].wait_recv()
        encode(jnp.where(broken, fix[a], own[a]), wins[a].at[0])
        got.append({d: ship(wins[a].at[0], wins[a].at[d], lower(d)) for d in (1, 3, 4)})

    grad_in.wait()
    kept.append(local(gv, gwin_ref.at[0]))
    step = 16

    def add_rows(i, total):
        x = gv[pl.ds(pl.multiple_of(i * step, step), step), :].astype(jnp.float32)
        return total + fold(x * x)

    part_one[0] = lax.fori_loop(0, gv.shape[0] // step, add_rows, jnp.zeros((8, LANES), jnp.float32))
    ones = [ship(part_one.at[0], part_one.at[d], lower(d)) for d in range(1, 4)]

    for c in range(1, CHUNKS):
        send_gradient(c)

    for a in range(3):
        got[a][1].wait_recv()
        got[a][2] = ship(wins[a].at[1, :, left], wins[a].at[2, :, left], lower(1))
        got[a][3].wait_recv()
        got[a][5] = ship(wins[a].at[3, :, right], wins[a].at[2, :, right], higher(1))

    for copy in ones:
        copy.wait_recv()
    part_two[0] = part_one[0] + part_one[1] + part_one[2] + part_one[3]
    twos = [ship(part_two.at[0], part_two.at[k + 1], lower(d)) for k, d in enumerate(STAGE_TWO)]

    up, down, across = [], [], []
    for a in range(3):
        for d in (4, 2, 5):
            got[a][d].wait_recv()
        for s in range(SLOTS):
            sel[a, s] = wins[a][gaps[s]]
        mine = gat_ref.at[a, :, piece(island)]
        up.append(ship(sel.at[a], mine, chip_y(1), lands=gat_ref.at[a, :, piece(along_y(-1))]))
        down.append(ship(sel.at[a], mine, chip_y(-1), lands=gat_ref.at[a, :, piece(along_y(1))]))
        across.append(ship(sel.at[a], mine, to_partner, lands=gat_ref.at[a, :, piece(partner)]))
        kept.append(local(sel.at[a], mine))

    grad_rest, grad_three = [], []
    for c in range(CHUNKS):
        grad_four[c].wait_recv()
        grad_three.append(ship(gwin_ref.at[4, gone[c]], gwin_ref.at[3, gone[c]], higher(1)))
        grad_one[c].wait_recv()
        if c < CHUNKS // 2:
            grad_rest.append(ship(gwin_ref.at[1, gone[c]], gwin_ref.at[2, gone[c]], lower(1)))

    partner_y = [lax.rem(partner + REP + 2 * dy, REP) for dy in range(4)]

    def cross(a, dy):
        theirs = gat_ref.at[a, :, piece(along_y(dy))]
        across.append(ship(theirs, theirs, to_partner, lands=gat_ref.at[a, :, piece(partner_y[dy])]))

    far = []
    for a in range(3):
        up[a].wait_recv()
        theirs = gat_ref.at[a, :, piece(along_y(-1)), left]
        far.append(ship(theirs, theirs, chip_y(1), lands=gat_ref.at[a, :, piece(along_y(2)), left]))
        down[a].wait_recv()
        theirs = gat_ref.at[a, :, piece(along_y(1)), right]
        far.append(ship(theirs, theirs, chip_y(-1), lands=gat_ref.at[a, :, piece(along_y(2)), right]))
        cross(a, 3)
        cross(a, 1)
    for c in range(CHUNKS):
        grad_three[c].wait_recv()
        if c >= CHUNKS // 2:
            grad_rest.append(ship(gwin_ref.at[3, gone[c]], gwin_ref.at[2, gone[c]], higher(1)))
    for a in range(3):
        far[2 * a].wait_recv()
        far[2 * a + 1].wait_recv()
        cross(a, 2)

    for copy in twos:
        copy.wait_recv()
    total = part_two[0]
    for k in range(1, len(STAGE_TWO) + 1):
        total = total + part_two[k]
    norm_ref[...] = total

    for copy in (*grad_rest, *across):
        copy.wait_recv()
    for copy in sent:
        copy.wait_send()
    for copy in kept:
        copy.wait()


def update_kernel(limit, meta_ref, norm_ref, gat_ref, g_ref, w_out, m_out, v_out, factor_ref):
    slot, part = pl.program_id(0), pl.program_id(1)

    @pl.when(jnp.logical_and(slot == 0, part == 0))
    def _():
        norm_sum = jnp.sum(norm_ref[...], keepdims=True)
        factor_ref[...] = jnp.broadcast_to(jnp.minimum(1.0, limit / (jnp.sqrt(norm_sum) + 1e-06)), factor_ref.shape)

    @pl.when(slot < meta_ref[0])
    def _():
        factor = factor_ref[0:1, 0:1]
        params, moment_one, moment_two = (decode(gat_ref[a, 0]) for a in range(3))
        clipped = g_ref[0].astype(jnp.float32) * factor
        one_new = beta_first * moment_one + (1.0 - beta_first) * clipped
        two_new = beta_second * moment_two + (1.0 - beta_second) * clipped * clipped
        step_dir = one_new / bias_first / (jnp.sqrt(two_new / bias_second) + eps_adam)
        w_out[...] = params - learn_rate * (step_dir + weight_decay * params)
        m_out[...] = one_new
        v_out[...] = two_new

    @pl.when(slot >= meta_ref[0])
    def _():
        for out in (w_out, m_out, v_out):
            out[...] = jnp.zeros_like(out)


def on_device(shard_lost, new_blocks, weights, first_moment, second_moment, gradient):
    _, block, ff = weights.shape
    rows = block // REP
    width = ff + LANES
    f32 = jnp.float32
    vmem, anywhere = pl.BlockSpec(memory_space=pltpu.VMEM), pl.BlockSpec(memory_space=pl.ANY)
    smem = pl.BlockSpec(memory_space=pltpu.SMEM)
    hbm = pl.BlockSpec(memory_space=pltpu.HBM)
    gat, gwin, norm, meta = pl.pallas_call(
        gather_kernel,
        out_shape=(
            jax.ShapeDtypeStruct((3, SLOTS, block, width), jnp.int16),
            jax.ShapeDtypeStruct((SHIFT + 1, block, ff), jnp.bfloat16),
            jax.ShapeDtypeStruct((8, 128), f32),
            jax.ShapeDtypeStruct((8,), jnp.int32),
        ),
        in_specs=[hbm] * 6,
        out_specs=(anywhere, anywhere, vmem, smem),
        scratch_shapes=[
            pltpu.SMEM(shard_lost.shape, jnp.int32),
            pltpu.SMEM(new_blocks.shape, jnp.int32),
            pltpu.VMEM((3, rows, ff), f32),
            pltpu.VMEM((3, rows, ff), f32),
            *[pltpu.VMEM((SHIFT + 1, rows, width), jnp.int16)] * 3,
            pltpu.VMEM((3, SLOTS, rows, width), jnp.int16),
            pltpu.VMEM((block, ff), jnp.bfloat16),
            pltpu.VMEM((4, 8, LANES), f32),
            pltpu.VMEM((8, 8, LANES), f32),
            pltpu.SemaphoreType.DMA((10,)),
            pltpu.SemaphoreType.DMA((72,)),
            pltpu.SemaphoreType.DMA((72,)),
        ],
        compiler_params=pltpu.CompilerParams(
            collective_id=0, has_side_effects=True, vmem_limit_bytes=24 * 2**20
        ),
        name="gather_blocks",
    )(shard_lost, new_blocks, weights[0], first_moment[0], second_moment[0], gradient[0])

    chunk = 64
    parts = block // chunk

    def source(slot, part, meta_ref):
        last = jnp.maximum(meta_ref[0], 1) - 1
        return jnp.minimum(slot, last), jnp.where(slot > last, parts - 1, part)

    def gat_map(slot, part, meta_ref):
        s, i = source(slot, part, meta_ref)
        return 0, s, i, 0

    def grad_map(slot, part, meta_ref):
        s, i = source(slot, part, meta_ref)
        return meta_ref[1 + s], i, 0

    out_spec = pl.BlockSpec((chunk, ff), lambda slot, part, meta_ref: (slot * parts + part, 0))
    limit = 0.5 * math.sqrt(block * WIDE * ff)
    outs = pl.pallas_call(
        functools.partial(update_kernel, limit),
        out_shape=[jax.ShapeDtypeStruct((SLOTS * block, ff), f32)] * 3,
        grid_spec=pltpu.PrefetchScalarGridSpec(
            num_scalar_prefetch=1,
            grid=(SLOTS, parts),
            in_specs=[
                pl.BlockSpec((8, 128), lambda slot, part, meta_ref: (0, 0)),
                pl.BlockSpec((3, 1, chunk, width), gat_map),
                pl.BlockSpec((1, chunk, ff), grad_map),
            ],
            out_specs=[out_spec] * 3,
            scratch_shapes=[pltpu.VMEM((8, 128), f32)],
        ),
        compiler_params=pltpu.CompilerParams(vmem_limit_bytes=24 * 2**20),
        name="adam_update",
    )(meta, norm, gat, gwin)
    return tuple(out[None] for out in outs)


def solution(mesh):
    split = P("rep", "wide", None)
    return jax.shard_map(
        on_device,
        mesh=mesh,
        in_specs=(P(), P(), split, split, split, split),
        out_specs=(split, split, split),
        check_vma=False,
    )
```

```python
import functools
import math

import jax
import jax.numpy as jnp
from jax import lax
from jax.experimental import pallas as pl
from jax.experimental.pallas import tpu as pltpu
from jax.sharding import PartitionSpec as P

beta_first = 0.9
beta_second = 0.95
bias_first = 1.0 - 0.9**20
bias_second = 1.0 - 0.95**20
learn_rate = 0.01
weight_decay = 0.1
eps_adam = 1e-08

WIDE = 32
REP = 8
SHIFT = 4
SLOTS = 3
LANES = 128
TOP = 32767.0
CHUNKS = 4
STAGE_TWO = tuple(range(4, WIDE, 4))
MESH = pl.DeviceIdType.MESH


def encode(x, out):
    size = jnp.abs(x)
    most = jnp.clip(jnp.max(size, axis=1, keepdims=True), 2.0**-120, 2.0**120)
    exponent = jnp.ceil(jnp.log2(most))
    code = jnp.minimum(jnp.round(jnp.sqrt(size * jnp.exp2(-exponent)) * TOP), TOP)
    code = jnp.where(x < 0, -code, code)
    out[:, : x.shape[1]] = code.astype(jnp.int32).astype(jnp.int16)
    tail = jnp.broadcast_to(exponent, (x.shape[0], LANES))
    out[:, x.shape[1] :] = tail.astype(jnp.int32).astype(jnp.int16)


def decode(x):
    columns = x.shape[1] - LANES
    code = x[:, :columns].astype(jnp.int32).astype(jnp.float32)
    scale = jnp.exp2(x[:, columns:].astype(jnp.int32).astype(jnp.float32)) * (1.0 / TOP**2)
    return code * jnp.abs(code) * jnp.concatenate([scale] * (columns // LANES), axis=1)


def fold(squares):
    top = squares[:8] + squares[8:]
    parts = [top[:, LANES * c : LANES * (c + 1)] for c in range(top.shape[1] // LANES)]
    while len(parts) > 1:
        parts = [sum(parts[i : i + 2][1:], parts[i]) for i in range(0, len(parts), 2)]
    return parts[0]


def gather_kernel(
    lost_hbm, blocks_hbm, w_ref, m_ref, v_ref, g_ref,
    gat_ref, gwin_ref, norm_ref, meta_ref,
    lost_ref, blocks_ref, own, fix, win_w, win_m, win_v, sel, gv, part_one, part_two, loc, out_sem, in_sem,
):
    arrays = (w_ref, m_ref, v_ref)
    wins = (win_w, win_m, win_v)
    rows = own.shape[1]
    island = lax.axis_index("rep")
    shard = lax.axis_index("wide")
    partner = island + 1 - 2 * lax.rem(island, 2)
    width = sel.shape[3]
    middle = width // LANES // 2 * LANES
    left, right = pl.ds(0, middle), pl.ds(middle, width - middle)
    to_partner = {"rep": partner, "wide": shard}
    used = {"remote": 0, "local": 0}

    def lower(d):
        return {"rep": island, "wide": lax.rem(shard + WIDE - d, WIDE)}

    def higher(d):
        return {"rep": island, "wide": lax.rem(shard + d, WIDE)}

    def along_y(dy):
        return lax.rem(island + REP + 2 * dy, REP)

    def chip_y(dy):
        return {"rep": along_y(dy), "wide": shard}

    def piece(p):
        return pl.ds(pl.multiple_of(p * rows, rows), rows)

    def send(src, dst, where, lands=None):
        k = used["remote"]
        used["remote"] = k + 1
        copy = pltpu.make_async_remote_copy(src, dst, out_sem.at[k], in_sem.at[k], device_id=where, device_id_type=MESH)
        copy.start()
        if lands is None:
            return copy, copy
        return copy, pltpu.make_async_remote_copy(
            src, lands, out_sem.at[k], in_sem.at[k], device_id=where, device_id_type=MESH
        )

    def local(src, dst):
        k = used["local"]
        used["local"] = k + 1
        copy = pltpu.make_async_copy(src, dst, loc.at[k])
        copy.start()
        return copy

    sent, kept = [], []

    def ship(*args, **kwargs):
        copy, lands = send(*args, **kwargs)
        sent.append(copy)
        return lands

    grad_in = local(g_ref, gv)
    own_in = [local(arrays[a].at[piece(island)], own.at[a]) for a in range(3)]
    lost_in, blocks_in = local(lost_hbm, lost_ref), local(blocks_hbm, blocks_ref)

    barrier = pltpu.get_barrier_semaphore()
    offsets = (1, 2, 3, *STAGE_TWO, WIDE - 1)
    greeted = [*(higher(d) for d in offsets), chip_y(1), chip_y(-1), to_partner]
    for device in greeted:
        pl.semaphore_signal(barrier, inc=1, device_id=device, device_id_type=MESH)
    pl.semaphore_wait(barrier, len(greeted))

    mend = [ship(arrays[a].at[piece(partner)], fix.at[a], to_partner) for a in range(3)]

    gstep = gv.shape[0] // CHUNKS
    gone = [pl.ds(c * gstep, gstep) for c in range(CHUNKS)]
    grads = {1: [], 2: [], 3: [], 4: []}

    def send_gradient(d, c):
        grads[d].append(ship(g_ref.at[gone[c]], gwin_ref.at[d, gone[c]], lower(d)))

    def relay_gradient(c):
        grads[4][c].wait_recv()
        grads[3].append(ship(gwin_ref.at[4, gone[c]], gwin_ref.at[3, gone[c]], higher(1)))

    send_gradient(4, 0)
    send_gradient(2, 0)

    lost_in.wait()
    blocks_in.wait()
    first = jnp.int32(0)
    count = jnp.int32(0)
    for k in range(blocks_ref.shape[0]):
        n = blocks_ref[k]
        first = first + jnp.where(k < shard, n, 0)
        count = count + jnp.where(k == shard, n, 0)
    gaps = [jnp.clip(first + s - shard, 0, SHIFT) for s in range(SLOTS)]
    meta_ref[0] = count
    for s in range(SLOTS):
        meta_ref[1 + s] = gaps[s]
    broken = lost_ref[island] == shard

    got = []
    for a in range(3):
        own_in[a].wait()
        mend[a].wait_recv()
        encode(jnp.where(broken, fix[a], own[a]), wins[a].at[0])
        got.append({d: ship(wins[a].at[0], wins[a].at[d], lower(d)) for d in (1, 3, 4)})

    grad_in.wait()
    kept.append(local(gv, gwin_ref.at[0]))
    step = 16

    def add_rows(i, total):
        x = gv[pl.ds(pl.multiple_of(i * step, step), step), :].astype(jnp.float32)
        return total + fold(x * x)

    part_one[0] = lax.fori_loop(0, gv.shape[0] // step, add_rows, jnp.zeros((8, LANES), jnp.float32))
    ones = [ship(part_one.at[0], part_one.at[d], lower(d)) for d in range(1, 4)]

    for a in range(3):
        got[a][1].wait_recv()
        got[a][2] = ship(wins[a].at[1, :, left], wins[a].at[2, :, left], lower(1))
        got[a][3].wait_recv()
        got[a][5] = ship(wins[a].at[3, :, right], wins[a].at[2, :, right], higher(1))

    send_gradient(4, 1)
    send_gradient(1, 0)
    send_gradient(2, 1)

    up, down, across = [], [], []
    for a in range(3):
        for d in (4, 2, 5):
            got[a][d].wait_recv()
        for s in range(SLOTS):
            sel[a, s] = wins[a][gaps[s]]
        mine = gat_ref.at[a, :, piece(island)]
        up.append(ship(sel.at[a], mine, chip_y(1), lands=gat_ref.at[a, :, piece(along_y(-1))]))
        down.append(ship(sel.at[a], mine, chip_y(-1), lands=gat_ref.at[a, :, piece(along_y(1))]))
        across.append(ship(sel.at[a], mine, to_partner, lands=gat_ref.at[a, :, piece(partner)]))
        kept.append(local(sel.at[a], mine))

    relay_gradient(0)
    for c in range(2, CHUNKS):
        send_gradient(4, c)
        send_gradient(1, c - 1)
        send_gradient(2, c)
    send_gradient(1, CHUNKS - 1)

    for copy in ones:
        copy.wait_recv()
    part_two[0] = part_one[0] + part_one[1] + part_one[2] + part_one[3]
    twos = [ship(part_two.at[0], part_two.at[k + 1], lower(d)) for k, d in enumerate(STAGE_TWO)]

    partner_y = [lax.rem(partner + REP + 2 * dy, REP) for dy in range(4)]

    def cross(a, dy):
        theirs = gat_ref.at[a, :, piece(along_y(dy))]
        across.append(ship(theirs, theirs, to_partner, lands=gat_ref.at[a, :, piece(partner_y[dy])]))

    far = []
    for a in range(3):
        relay_gradient(a + 1)
        up[a].wait_recv()
        theirs = gat_ref.at[a, :, piece(along_y(-1)), left]
        far.append(ship(theirs, theirs, chip_y(1), lands=gat_ref.at[a, :, piece(along_y(2)), left]))
        down[a].wait_recv()
        theirs = gat_ref.at[a, :, piece(along_y(1)), right]
        far.append(ship(theirs, theirs, chip_y(-1), lands=gat_ref.at[a, :, piece(along_y(2)), right]))
        cross(a, 3)
        cross(a, 1)
    for a in range(3):
        far[2 * a].wait_recv()
        far[2 * a + 1].wait_recv()
        cross(a, 2)

    for copy in twos:
        copy.wait_recv()
    total = part_two[0]
    for k in range(1, len(STAGE_TWO) + 1):
        total = total + part_two[k]
    norm_ref[...] = total

    for copy in (*grads[1], *grads[2], *grads[3], *across):
        copy.wait_recv()
    for copy in sent:
        copy.wait_send()
    for copy in kept:
        copy.wait()


def update_kernel(limit, meta_ref, norm_ref, gat_ref, g_ref, w_out, m_out, v_out, factor_ref):
    slot, part = pl.program_id(0), pl.program_id(1)

    @pl.when(jnp.logical_and(slot == 0, part == 0))
    def _():
        norm_sum = jnp.sum(norm_ref[...], keepdims=True)
        factor_ref[...] = jnp.broadcast_to(jnp.minimum(1.0, limit / (jnp.sqrt(norm_sum) + 1e-06)), factor_ref.shape)

    @pl.when(slot < meta_ref[0])
    def _():
        factor = factor_ref[0:1, 0:1]
        params, moment_one, moment_two = (decode(gat_ref[a, 0]) for a in range(3))
        clipped = g_ref[0].astype(jnp.float32) * factor
        one_new = beta_first * moment_one + (1.0 - beta_first) * clipped
        two_new = beta_second * moment_two + (1.0 - beta_second) * clipped * clipped
        step_dir = one_new / bias_first / (jnp.sqrt(two_new / bias_second) + eps_adam)
        w_out[...] = params - learn_rate * (step_dir + weight_decay * params)
        m_out[...] = one_new
        v_out[...] = two_new

    @pl.when(slot >= meta_ref[0])
    def _():
        for out in (w_out, m_out, v_out):
            out[...] = jnp.zeros_like(out)


def on_device(shard_lost, new_blocks, weights, first_moment, second_moment, gradient):
    _, block, ff = weights.shape
    rows = block // REP
    width = ff + LANES
    f32 = jnp.float32
    vmem, anywhere = pl.BlockSpec(memory_space=pltpu.VMEM), pl.BlockSpec(memory_space=pl.ANY)
    smem = pl.BlockSpec(memory_space=pltpu.SMEM)
    hbm = pl.BlockSpec(memory_space=pltpu.HBM)
    gat, gwin, norm, meta = pl.pallas_call(
        gather_kernel,
        out_shape=(
            jax.ShapeDtypeStruct((3, SLOTS, block, width), jnp.int16),
            jax.ShapeDtypeStruct((SHIFT + 1, block, ff), jnp.bfloat16),
            jax.ShapeDtypeStruct((8, 128), f32),
            jax.ShapeDtypeStruct((8,), jnp.int32),
        ),
        in_specs=[hbm] * 6,
        out_specs=(anywhere, anywhere, vmem, smem),
        scratch_shapes=[
            pltpu.SMEM(shard_lost.shape, jnp.int32),
            pltpu.SMEM(new_blocks.shape, jnp.int32),
            pltpu.VMEM((3, rows, ff), f32),
            pltpu.VMEM((3, rows, ff), f32),
            *[pltpu.VMEM((SHIFT + 1, rows, width), jnp.int16)] * 3,
            pltpu.VMEM((3, SLOTS, rows, width), jnp.int16),
            pltpu.VMEM((block, ff), jnp.bfloat16),
            pltpu.VMEM((4, 8, LANES), f32),
            pltpu.VMEM((8, 8, LANES), f32),
            pltpu.SemaphoreType.DMA((10,)),
            pltpu.SemaphoreType.DMA((72,)),
            pltpu.SemaphoreType.DMA((72,)),
        ],
        compiler_params=pltpu.CompilerParams(
            collective_id=0, has_side_effects=True, vmem_limit_bytes=60 * 2**20
        ),
        name="gather_blocks",
    )(shard_lost, new_blocks, weights[0], first_moment[0], second_moment[0], gradient[0])

    chunk = 64
    parts = block // chunk

    def source(slot, part, meta_ref):
        last = jnp.maximum(meta_ref[0], 1) - 1
        return jnp.minimum(slot, last), jnp.where(slot > last, parts - 1, part)

    def gat_map(slot, part, meta_ref):
        s, i = source(slot, part, meta_ref)
        return 0, s, i, 0

    def grad_map(slot, part, meta_ref):
        s, i = source(slot, part, meta_ref)
        return meta_ref[1 + s], i, 0

    out_spec = pl.BlockSpec((chunk, ff), lambda slot, part, meta_ref: (slot * parts + part, 0))
    limit = 0.5 * math.sqrt(block * WIDE * ff)
    outs = pl.pallas_call(
        functools.partial(update_kernel, limit),
        out_shape=[jax.ShapeDtypeStruct((SLOTS * block, ff), f32)] * 3,
        grid_spec=pltpu.PrefetchScalarGridSpec(
            num_scalar_prefetch=1,
            grid=(SLOTS, parts),
            in_specs=[
                pl.BlockSpec((8, 128), lambda slot, part, meta_ref: (0, 0)),
                pl.BlockSpec((3, 1, chunk, width), gat_map),
                pl.BlockSpec((1, chunk, ff), grad_map),
            ],
            out_specs=[out_spec] * 3,
            scratch_shapes=[pltpu.VMEM((8, 128), f32)],
        ),
        compiler_params=pltpu.CompilerParams(vmem_limit_bytes=60 * 2**20),
        name="adam_update",
    )(meta, norm, gat, gwin)
    return tuple(out[None] for out in outs)


def solution(mesh):
    split = P("rep", "wide", None)
    return jax.shard_map(
        on_device,
        mesh=mesh,
        in_specs=(P(), P(), split, split, split, split),
        out_specs=(split, split, split),
        check_vma=False,
    )
```

```python
import functools
import math

import jax
import jax.numpy as jnp
from jax import lax
from jax.experimental import pallas as pl
from jax.experimental.pallas import tpu as pltpu
from jax.sharding import PartitionSpec as P

beta_first = 0.9
beta_second = 0.95
bias_first = 1.0 - 0.9**20
bias_second = 1.0 - 0.95**20
learn_rate = 0.01
weight_decay = 0.1
eps_adam = 1e-08

WIDE = 32
REP = 8
ROW = 4
SHIFT = 4
SLOTS = 3
LANES = 128
TOP = 32767.0
CHUNKS = 4
STAGE_TWO = tuple(range(ROW, WIDE, ROW))
MESH = pl.DeviceIdType.MESH


def encode(x, out):
    size = jnp.abs(x)
    most = jnp.clip(jnp.max(size, axis=1, keepdims=True), 2.0**-120, 2.0**120)
    exponent = jnp.ceil(jnp.log2(most))
    code = jnp.minimum(jnp.round(jnp.sqrt(size * jnp.exp2(-exponent)) * TOP), TOP)
    code = jnp.where(x < 0, -code, code)
    out[:, : x.shape[1]] = code.astype(jnp.int32).astype(jnp.int16)
    tail = jnp.broadcast_to(exponent, (x.shape[0], LANES))
    out[:, x.shape[1] :] = tail.astype(jnp.int32).astype(jnp.int16)


def decode(x):
    columns = x.shape[1] - LANES
    code = x[:, :columns].astype(jnp.int32).astype(jnp.float32)
    scale = jnp.exp2(x[:, columns:].astype(jnp.int32).astype(jnp.float32)) * (1.0 / TOP**2)
    return code * jnp.abs(code) * jnp.concatenate([scale] * (columns // LANES), axis=1)


def fold(squares):
    top = squares[:8] + squares[8:]
    parts = [top[:, LANES * c : LANES * (c + 1)] for c in range(top.shape[1] // LANES)]
    while len(parts) > 1:
        parts = [sum(parts[i : i + 2][1:], parts[i]) for i in range(0, len(parts), 2)]
    return parts[0]


def gather_kernel(
    lost_hbm, blocks_hbm, w_ref, m_ref, v_ref, g_ref,
    gat_ref, gwin_ref, norm_ref, meta_ref,
    lost_ref, blocks_ref, own, fix, win_w, win_m, win_v, sel, gv, part_one, part_two, loc, out_sem, in_sem,
):
    arrays = (w_ref, m_ref, v_ref)
    wins = (win_w, win_m, win_v)
    rows = own.shape[1]
    island = lax.axis_index("rep")
    shard = lax.axis_index("wide")
    partner = island + 1 - 2 * lax.rem(island, 2)
    width = sel.shape[3]
    middle = width // LANES // 2 * LANES
    left, right = pl.ds(0, middle), pl.ds(middle, width - middle)
    to_partner = {"rep": partner, "wide": shard}
    used = {"remote": 0, "local": 0}

    def lower(d):
        return {"rep": island, "wide": lax.rem(shard + WIDE - d, WIDE)}

    def higher(d):
        return {"rep": island, "wide": lax.rem(shard + d, WIDE)}

    column = lax.rem(shard, ROW)

    def in_row(d):
        return {"rep": island, "wide": shard - column + lax.rem(column + ROW - d, ROW)}

    def along_y(dy):
        return lax.rem(island + REP + 2 * dy, REP)

    def chip_y(dy):
        return {"rep": along_y(dy), "wide": shard}

    def piece(p):
        return pl.ds(pl.multiple_of(p * rows, rows), rows)

    def maker(where):
        k = used["remote"]
        used["remote"] = k + 1

        def make(src, dst):
            return pltpu.make_async_remote_copy(
                src, dst, out_sem.at[k], in_sem.at[k], device_id=where, device_id_type=MESH
            )

        return make

    def local(src, dst):
        k = used["local"]
        used["local"] = k + 1
        copy = pltpu.make_async_copy(src, dst, loc.at[k])
        copy.start()
        return copy

    sent, kept = [], []

    def ship(src, dst, where, lands=None):
        make = maker(where)
        copy = make(src, dst)
        copy.start()
        sent.append(copy)
        return copy if lands is None else make(src, lands)

    def ship_in_row(d, own_src, above_src, dst):
        make = maker(in_row(d))
        copy = make(own_src, dst)
        sent.append(copy)

        @pl.when(column >= d)
        def _():
            copy.start()

        def go():
            @pl.when(column < d)
            def _():
                make(above_src, dst).start()

        return copy, go

    grad_in = local(g_ref, gv)
    own_in = [local(arrays[a].at[piece(island)], own.at[a]) for a in range(3)]
    lost_in, blocks_in = local(lost_hbm, lost_ref), local(blocks_hbm, blocks_ref)

    barrier = pltpu.get_barrier_semaphore()
    offsets = (1, *STAGE_TWO, WIDE - 1)
    greeted = [*(higher(d) for d in offsets), *(in_row(d) for d in range(1, ROW)), chip_y(1), chip_y(-1), to_partner]
    for device in greeted:
        pl.semaphore_signal(barrier, inc=1, device_id=device, device_id_type=MESH)
    pl.semaphore_wait(barrier, len(greeted))

    mend = [ship(arrays[a].at[piece(partner)], fix.at[a], to_partner) for a in range(3)]

    gstep = gv.shape[0] // CHUNKS
    gone = [pl.ds(c * gstep, gstep) for c in range(CHUNKS)]
    grads = {d: [None] * CHUNKS for d in range(1, SHIFT + 1)}
    grad_go = [None] * CHUNKS

    def grad_first(c):
        rows_c = gone[c]
        grads[4][c] = ship(g_ref.at[rows_c], gwin_ref.at[4, rows_c], lower(4))
        grad_go[c] = []
        for d in (1, 3):
            grads[d][c], go = ship_in_row(d, g_ref.at[rows_c], gwin_ref.at[4, rows_c], gwin_ref.at[d, rows_c])
            grad_go[c].append(go)

    def grad_second(c):
        grads[4][c].wait_recv()
        for go in grad_go[c]:
            go()

    def grad_two(c, d):
        grads[d][c].wait_recv()
        to = lower(1) if d == 1 else higher(1)
        grads[2][c] = ship(gwin_ref.at[d, gone[c]], gwin_ref.at[2, gone[c]], to)

    grad_first(0)

    lost_in.wait()
    blocks_in.wait()
    first = jnp.int32(0)
    count = jnp.int32(0)
    for k in range(blocks_ref.shape[0]):
        n = blocks_ref[k]
        first = first + jnp.where(k < shard, n, 0)
        count = count + jnp.where(k == shard, n, 0)
    gaps = [jnp.clip(first + s - shard, 0, SHIFT) for s in range(SLOTS)]
    meta_ref[0] = count
    for s in range(SLOTS):
        meta_ref[1 + s] = gaps[s]
    broken = lost_ref[island] == shard

    windows, ring, far, across = [], [], [], []

    def code(a):
        own_in[a].wait()
        mend[a].wait_recv()
        encode(jnp.where(broken, fix[a], own[a]), wins[a].at[0])

    def first(a):
        win = wins[a]
        down = ship(win.at[0], win.at[4], lower(4))
        windows.append((down, [ship_in_row(d, win.at[0], win.at[4], win.at[d]) for d in (2, 1, 3)]))

    def second(a):
        windows[a][0].wait_recv()
        for _, go in windows[a][1]:
            go()

    def pick(a):
        for lands, _ in windows[a][1]:
            lands.wait_recv()
        for s in range(SLOTS):
            sel[a, s] = wins[a][gaps[s]]
        mine = gat_ref.at[a, :, piece(island)]
        ring.append(
            (
                ship(sel.at[a], mine, chip_y(1), lands=gat_ref.at[a, :, piece(along_y(-1))]),
                ship(sel.at[a], mine, chip_y(-1), lands=gat_ref.at[a, :, piece(along_y(1))]),
            )
        )
        across.append(ship(sel.at[a], mine, to_partner, lands=gat_ref.at[a, :, piece(partner)]))
        kept.append(local(sel.at[a], mine))

    def cross(a, dy):
        theirs = gat_ref.at[a, :, piece(along_y(dy))]
        lands = gat_ref.at[a, :, piece(lax.rem(partner + REP + 2 * dy, REP))]
        across.append(ship(theirs, theirs, to_partner, lands=lands))

    def pass_on(a):
        halves = []
        for copy, dy, half in ((ring[a][0], 1, left), (ring[a][1], -1, right)):
            copy.wait_recv()
            theirs = gat_ref.at[a, :, piece(along_y(-dy)), half]
            halves.append(ship(theirs, theirs, chip_y(dy), lands=gat_ref.at[a, :, piece(along_y(2)), half]))
            cross(a, -dy)
        far.append(halves)

    def close(a):
        for copy in far[a]:
            copy.wait_recv()
        cross(a, 2)

    code(0)
    first(0)
    code(1)
    first(1)
    code(2)
    second(0)

    grad_in.wait()
    kept.append(local(gv, gwin_ref.at[0]))
    step = 16

    def add_rows(i, total):
        x = gv[pl.ds(pl.multiple_of(i * step, step), step), :].astype(jnp.float32)
        return total + fold(x * x)

    part_one[0] = lax.fori_loop(0, gv.shape[0] // step, add_rows, jnp.zeros((8, LANES), jnp.float32))
    ones = [ship(part_one.at[0], part_one.at[d], in_row(d)) for d in range(1, ROW)]

    pick(0)
    first(2)
    second(1)
    for c in range(1, CHUNKS):
        grad_first(c)
    grad_second(0)
    pick(1)
    second(2)
    for copy in ones:
        copy.wait_recv()
    part_two[0] = part_one[0] + part_one[1] + part_one[2] + part_one[3]
    twos = [ship(part_two.at[0], part_two.at[k + 1], lower(d)) for k, d in enumerate(STAGE_TWO)]
    grad_second(1)
    grad_two(0, 3)
    pick(2)
    grad_second(2)
    grad_two(2, 1)
    pass_on(0)
    grad_two(1, 3)
    grad_second(3)
    pass_on(1)
    grad_two(3, 1)
    pass_on(2)
    close(0)
    close(1)
    close(2)

    for copy in twos:
        copy.wait_recv()
    total = part_two[0]
    for k in range(1, len(STAGE_TWO) + 1):
        total = total + part_two[k]
    norm_ref[...] = total

    for copy in (*grads[1][:2], *grads[2], *grads[3][2:], *across):
        copy.wait_recv()
    for copy in sent:
        copy.wait_send()
    for copy in kept:
        copy.wait()


def update_kernel(limit, meta_ref, norm_ref, gat_ref, g_ref, w_out, m_out, v_out, factor_ref):
    slot, part = pl.program_id(0), pl.program_id(1)

    @pl.when(jnp.logical_and(slot == 0, part == 0))
    def _():
        norm_sum = jnp.sum(norm_ref[...], keepdims=True)
        factor_ref[...] = jnp.broadcast_to(jnp.minimum(1.0, limit / (jnp.sqrt(norm_sum) + 1e-06)), factor_ref.shape)

    @pl.when(slot < meta_ref[0])
    def _():
        factor = factor_ref[0:1, 0:1]
        params, moment_one, moment_two = (decode(gat_ref[a, 0]) for a in range(3))
        clipped = g_ref[0].astype(jnp.float32) * factor
        one_new = beta_first * moment_one + (1.0 - beta_first) * clipped
        two_new = beta_second * moment_two + (1.0 - beta_second) * clipped * clipped
        step_dir = one_new / bias_first / (jnp.sqrt(two_new / bias_second) + eps_adam)
        w_out[...] = params - learn_rate * (step_dir + weight_decay * params)
        m_out[...] = one_new
        v_out[...] = two_new

    @pl.when(slot >= meta_ref[0])
    def _():
        for out in (w_out, m_out, v_out):
            out[...] = jnp.zeros_like(out)


def on_device(shard_lost, new_blocks, weights, first_moment, second_moment, gradient):
    _, block, ff = weights.shape
    rows = block // REP
    width = ff + LANES
    f32 = jnp.float32
    vmem, anywhere = pl.BlockSpec(memory_space=pltpu.VMEM), pl.BlockSpec(memory_space=pl.ANY)
    smem = pl.BlockSpec(memory_space=pltpu.SMEM)
    hbm = pl.BlockSpec(memory_space=pltpu.HBM)
    gat, gwin, norm, meta = pl.pallas_call(
        gather_kernel,
        out_shape=(
            jax.ShapeDtypeStruct((3, SLOTS, block, width), jnp.int16),
            jax.ShapeDtypeStruct((SHIFT + 1, block, ff), jnp.bfloat16),
            jax.ShapeDtypeStruct((8, 128), f32),
            jax.ShapeDtypeStruct((8,), jnp.int32),
        ),
        in_specs=[hbm] * 6,
        out_specs=(anywhere, anywhere, vmem, smem),
        scratch_shapes=[
            pltpu.SMEM(shard_lost.shape, jnp.int32),
            pltpu.SMEM(new_blocks.shape, jnp.int32),
            pltpu.VMEM((3, rows, ff), f32),
            pltpu.VMEM((3, rows, ff), f32),
            *[pltpu.VMEM((SHIFT + 1, rows, width), jnp.int16)] * 3,
            pltpu.VMEM((3, SLOTS, rows, width), jnp.int16),
            pltpu.VMEM((block, ff), jnp.bfloat16),
            pltpu.VMEM((4, 8, LANES), f32),
            pltpu.VMEM((8, 8, LANES), f32),
            pltpu.SemaphoreType.DMA((10,)),
            pltpu.SemaphoreType.DMA((72,)),
            pltpu.SemaphoreType.DMA((72,)),
        ],
        compiler_params=pltpu.CompilerParams(
            collective_id=0, has_side_effects=True, vmem_limit_bytes=60 * 2**20
        ),
        name="gather_blocks",
    )(shard_lost, new_blocks, weights[0], first_moment[0], second_moment[0], gradient[0])

    chunk = 64
    parts = block // chunk

    def source(slot, part, meta_ref):
        last = jnp.maximum(meta_ref[0], 1) - 1
        return jnp.minimum(slot, last), jnp.where(slot > last, parts - 1, part)

    def gat_map(slot, part, meta_ref):
        s, i = source(slot, part, meta_ref)
        return 0, s, i, 0

    def grad_map(slot, part, meta_ref):
        s, i = source(slot, part, meta_ref)
        return meta_ref[1 + s], i, 0

    out_spec = pl.BlockSpec((chunk, ff), lambda slot, part, meta_ref: (slot * parts + part, 0))
    limit = 0.5 * math.sqrt(block * WIDE * ff)
    outs = pl.pallas_call(
        functools.partial(update_kernel, limit),
        out_shape=[jax.ShapeDtypeStruct((SLOTS * block, ff), f32)] * 3,
        grid_spec=pltpu.PrefetchScalarGridSpec(
            num_scalar_prefetch=1,
            grid=(SLOTS, parts),
            in_specs=[
                pl.BlockSpec((8, 128), lambda slot, part, meta_ref: (0, 0)),
                pl.BlockSpec((3, 1, chunk, width), gat_map),
                pl.BlockSpec((1, chunk, ff), grad_map),
            ],
            out_specs=[out_spec] * 3,
            scratch_shapes=[pltpu.VMEM((8, 128), f32)],
        ),
        compiler_params=pltpu.CompilerParams(vmem_limit_bytes=60 * 2**20),
        name="adam_update",
    )(meta, norm, gat, gwin)
    return tuple(out[None] for out in outs)


def solution(mesh):
    split = P("rep", "wide", None)
    return jax.shard_map(
        on_device,
        mesh=mesh,
        in_specs=(P(), P(), split, split, split, split),
        out_specs=(split, split, split),
        check_vma=False,
    )
```

```python
import functools
import math

import jax
import jax.numpy as jnp
from jax import lax
from jax.experimental import pallas as pl
from jax.experimental.pallas import tpu as pltpu
from jax.sharding import PartitionSpec as P

beta_first = 0.9
beta_second = 0.95
bias_first = 1.0 - 0.9**20
bias_second = 1.0 - 0.95**20
learn_rate = 0.01
weight_decay = 0.1
eps_adam = 1e-08

WIDE = 32
REP = 8
ROW = 4
SHIFT = 4
SLOTS = 3
LANES = 128
TOP = 32767.0
CHUNKS = 4
STEP = 32
STAGE_TWO = tuple(range(ROW, WIDE, ROW))
MESH = pl.DeviceIdType.MESH


def encode(x, out):
    size = jnp.abs(x)
    most = jnp.clip(jnp.max(size, axis=1, keepdims=True), 2.0**-120, 2.0**120)
    exponent = jnp.ceil(jnp.log2(most))
    code = jnp.minimum(jnp.round(jnp.sqrt(size * jnp.exp2(-exponent)) * TOP), TOP)
    code = jnp.where(x < 0, -code, code)
    out[:, : x.shape[1]] = code.astype(jnp.int32).astype(jnp.int16)
    tail = jnp.broadcast_to(exponent, (x.shape[0], LANES))
    out[:, x.shape[1] :] = tail.astype(jnp.int32).astype(jnp.int16)


def decode(x, times):
    columns = x.shape[1] - LANES
    code = x[:, :columns].astype(jnp.int32).astype(jnp.float32)
    scale = jnp.exp2(x[:, columns:].astype(jnp.int32).astype(jnp.float32)) * (times / TOP**2)
    return code * jnp.abs(code) * jnp.concatenate([scale] * (columns // LANES), axis=1)


def fold(squares):
    top = squares[:8] + squares[8:]
    parts = [top[:, LANES * c : LANES * (c + 1)] for c in range(top.shape[1] // LANES)]
    while len(parts) > 1:
        parts = [sum(parts[i : i + 2][1:], parts[i]) for i in range(0, len(parts), 2)]
    return parts[0]


def gather_kernel(
    lost_hbm, blocks_hbm, w_ref, m_ref, v_ref, g_ref,
    gat_ref, gwin_ref, norm_ref, meta_ref,
    lost_ref, blocks_ref, own, fix, win_w, win_m, win_v, sel, gv, part_one, part_two, loc, out_sem, in_sem,
):
    arrays = (w_ref, m_ref, v_ref)
    wins = (win_w, win_m, win_v)
    rows = own.shape[1]
    island = lax.axis_index("rep")
    shard = lax.axis_index("wide")
    partner = island + 1 - 2 * lax.rem(island, 2)
    width = sel.shape[3]
    middle = width // LANES // 2 * LANES
    left, right = pl.ds(0, middle), pl.ds(middle, width - middle)
    to_partner = {"rep": partner, "wide": shard}
    used = {"remote": 0, "local": 0}

    def lower(d):
        return {"rep": island, "wide": lax.rem(shard + WIDE - d, WIDE)}

    def higher(d):
        return {"rep": island, "wide": lax.rem(shard + d, WIDE)}

    column = lax.rem(shard, ROW)

    def in_row(d):
        return {"rep": island, "wide": shard - column + lax.rem(column + ROW - d, ROW)}

    def along_y(dy):
        return lax.rem(island + REP + 2 * dy, REP)

    def chip_y(dy):
        return {"rep": along_y(dy), "wide": shard}

    def piece(p):
        return pl.ds(pl.multiple_of(p * rows, rows), rows)

    def maker(where):
        k = used["remote"]
        used["remote"] = k + 1

        def make(src, dst):
            return pltpu.make_async_remote_copy(
                src, dst, out_sem.at[k], in_sem.at[k], device_id=where, device_id_type=MESH
            )

        return make

    def local(src, dst):
        k = used["local"]
        used["local"] = k + 1
        copy = pltpu.make_async_copy(src, dst, loc.at[k])
        copy.start()
        return copy

    sent, kept = [], []

    def ship(src, dst, where, lands=None):
        make = maker(where)
        copy = make(src, dst)
        copy.start()
        sent.append(copy)
        return copy if lands is None else make(src, lands)

    def ship_in_row(d, own_src, above_src, dst):
        make = maker(in_row(d))
        copy = make(own_src, dst)
        sent.append(copy)

        @pl.when(column >= d)
        def _():
            copy.start()

        def go():
            @pl.when(column < d)
            def _():
                make(above_src, dst).start()

        return copy, go

    grad_in = local(g_ref, gv)
    own_in = [local(arrays[a].at[piece(island)], own.at[a]) for a in range(3)]
    lost_in, blocks_in = local(lost_hbm, lost_ref), local(blocks_hbm, blocks_ref)

    barrier = pltpu.get_barrier_semaphore()
    offsets = (1, *STAGE_TWO, WIDE - 1)
    greeted = [*(higher(d) for d in offsets), *(in_row(d) for d in range(1, ROW)), chip_y(1), chip_y(-1), to_partner]
    for device in greeted:
        pl.semaphore_signal(barrier, inc=1, device_id=device, device_id_type=MESH)
    pl.semaphore_wait(barrier, len(greeted))

    mend = [ship(arrays[a].at[piece(partner)], fix.at[a], to_partner) for a in range(3)]

    gstep = gv.shape[0] // CHUNKS
    gone = [pl.ds(c * gstep, gstep) for c in range(CHUNKS)]
    grads = {d: [None] * CHUNKS for d in range(1, SHIFT + 1)}
    grad_go = [None] * CHUNKS

    def grad_first(c):
        rows_c = gone[c]
        grads[4][c] = ship(g_ref.at[rows_c], gwin_ref.at[4, rows_c], lower(4))
        grad_go[c] = []
        for d in (1, 3):
            grads[d][c], go = ship_in_row(d, g_ref.at[rows_c], gwin_ref.at[4, rows_c], gwin_ref.at[d, rows_c])
            grad_go[c].append(go)

    def grad_second(c):
        grads[4][c].wait_recv()
        for go in grad_go[c]:
            go()

    def grad_two(c, d):
        grads[d][c].wait_recv()
        to = lower(1) if d == 1 else higher(1)
        grads[2][c] = ship(gwin_ref.at[d, gone[c]], gwin_ref.at[2, gone[c]], to)

    grad_first(0)

    lost_in.wait()
    blocks_in.wait()
    first = jnp.int32(0)
    count = jnp.int32(0)
    for k in range(blocks_ref.shape[0]):
        n = blocks_ref[k]
        first = first + jnp.where(k < shard, n, 0)
        count = count + jnp.where(k == shard, n, 0)
    gaps = [jnp.clip(first + s - shard, 0, SHIFT) for s in range(SLOTS)]
    meta_ref[0] = count
    for s in range(SLOTS):
        meta_ref[1 + s] = gaps[s]
    broken = lost_ref[island] == shard

    windows, ring, far, across = [], [], [], []

    def code(a):
        own_in[a].wait()
        mend[a].wait_recv()
        encode(jnp.where(broken, fix[a], own[a]), wins[a].at[0])

    def first(a):
        win = wins[a]
        down = ship(win.at[0], win.at[4], lower(4))
        windows.append((down, [ship_in_row(d, win.at[0], win.at[4], win.at[d]) for d in (2, 1, 3)]))

    def second(a):
        windows[a][0].wait_recv()
        for _, go in windows[a][1]:
            go()

    def pick(a):
        for lands, _ in windows[a][1]:
            lands.wait_recv()
        for s in range(SLOTS):
            sel[a, s] = wins[a][gaps[s]]
        mine = gat_ref.at[a, :, piece(island)]
        ring.append(
            (
                ship(sel.at[a], mine, chip_y(1), lands=gat_ref.at[a, :, piece(along_y(-1))]),
                ship(sel.at[a], mine, chip_y(-1), lands=gat_ref.at[a, :, piece(along_y(1))]),
            )
        )
        across.append(ship(sel.at[a], mine, to_partner, lands=gat_ref.at[a, :, piece(partner)]))
        kept.append(local(sel.at[a], mine))

    def cross(a, dy):
        theirs = gat_ref.at[a, :, piece(along_y(dy))]
        lands = gat_ref.at[a, :, piece(lax.rem(partner + REP + 2 * dy, REP))]
        across.append(ship(theirs, theirs, to_partner, lands=lands))

    def pass_on(a):
        halves = []
        for copy, dy, half in ((ring[a][0], 1, left), (ring[a][1], -1, right)):
            copy.wait_recv()
            theirs = gat_ref.at[a, :, piece(along_y(-dy)), half]
            halves.append(ship(theirs, theirs, chip_y(dy), lands=gat_ref.at[a, :, piece(along_y(2)), half]))
            cross(a, -dy)
        far.append(halves)

    def close(a):
        for copy in far[a]:
            copy.wait_recv()
        cross(a, 2)

    code(0)
    first(0)
    code(1)
    first(1)
    code(2)
    second(0)

    grad_in.wait()
    kept.append(local(gv, gwin_ref.at[0]))
    step = 16

    def add_rows(i, total):
        x = gv[pl.ds(pl.multiple_of(i * step, step), step), :].astype(jnp.float32)
        return total + fold(x * x)

    part_one[0] = lax.fori_loop(0, gv.shape[0] // step, add_rows, jnp.zeros((8, LANES), jnp.float32))
    ones = [ship(part_one.at[0], part_one.at[d], in_row(d)) for d in range(1, ROW)]

    pick(0)
    first(2)
    second(1)
    grad_second(0)
    pick(1)
    second(2)
    for c in range(1, CHUNKS):
        grad_first(c)
    for copy in ones:
        copy.wait_recv()
    part_two[0] = part_one[0] + part_one[1] + part_one[2] + part_one[3]
    twos = [ship(part_two.at[0], part_two.at[k + 1], lower(d)) for k, d in enumerate(STAGE_TWO)]
    grad_two(0, 3)
    pick(2)
    grad_second(1)
    pass_on(0)
    grad_second(2)
    grad_two(1, 3)
    pass_on(1)
    grad_second(3)
    grad_two(2, 3)
    pass_on(2)
    grad_two(3, 1)
    close(0)
    close(1)
    close(2)

    for copy in twos:
        copy.wait_recv()
    total = part_two[0]
    for k in range(1, len(STAGE_TWO) + 1):
        total = total + part_two[k]
    norm_ref[...] = total

    for copy in (grads[1][0], grads[1][1], grads[1][2], grads[3][3], *grads[2], *across):
        copy.wait_recv()
    for copy in sent:
        copy.wait_send()
    for copy in kept:
        copy.wait()


def update_kernel(
    limit, meta_ref, norm_ref, gat_ref, gwin_ref, w_out, m_out, v_out,
    codes, grads, fresh, zeros, in_sem, grad_sem, out_sem, zero_sem,
):
    outs = (w_out, m_out, v_out)
    block = codes.shape[2]
    steps = block // STEP
    count = meta_ref[0]

    def fetch(s):
        copies = [pltpu.make_async_copy(gat_ref.at[a, s], codes.at[a, s], in_sem.at[a, s]) for a in range(3)]
        return (*copies, pltpu.make_async_copy(gwin_ref.at[meta_ref[1 + s]], grads.at[s], grad_sem.at[s]))

    def clear(s):
        return [pltpu.make_async_copy(zeros, outs[a].at[pl.ds(s * block, block)], zero_sem.at[a, s]) for a in range(3)]

    def give(a, s, i):
        rows = pl.ds(pl.multiple_of(i * STEP, STEP), STEP)
        there = pl.ds(pl.multiple_of(s * block + i * STEP, STEP), STEP)
        return pltpu.make_async_copy(fresh.at[a, s, rows], outs[a].at[there], out_sem.at[a, s, i])

    for s in range(SLOTS):

        @pl.when(s < count)
        def _(s=s):
            for copy in fetch(s):
                copy.start()

    zeros[...] = jnp.zeros_like(zeros)
    for s in range(SLOTS):

        @pl.when(s >= count)
        def _(s=s):
            for copy in clear(s):
                copy.start()

    norm_sum = jnp.sum(norm_ref[...], keepdims=True)
    factor = jnp.minimum(1.0, limit / (jnp.sqrt(norm_sum) + 1e-06))
    share_one = (1.0 - beta_first) * factor
    share_two = (1.0 - beta_second) * factor * factor

    for s in range(SLOTS):

        @pl.when(s < count)
        def _(s=s):
            for copy in fetch(s):
                copy.wait()

            def some_rows(i, carry):
                rows = pl.ds(pl.multiple_of(i * STEP, STEP), STEP)
                grad = grads[s, rows].astype(jnp.float32)
                one_new = decode(codes[1, s, rows], beta_first) + grad * share_one
                two_new = decode(codes[2, s, rows], beta_second) + grad * grad * share_two
                scaled = two_new * (1.0 / bias_second)
                step_dir = one_new * (learn_rate / bias_first) / (scaled * lax.rsqrt(scaled) + eps_adam)
                fresh[0, s, rows] = decode(codes[0, s, rows], 1.0 - learn_rate * weight_decay) - step_dir
                fresh[1, s, rows] = one_new
                fresh[2, s, rows] = two_new
                for a in range(3):
                    give(a, s, i).start()
                return carry

            lax.fori_loop(0, steps, some_rows, 0)

    for s in range(SLOTS):

        @pl.when(s < count)
        def _(s=s):
            for a in range(3):
                for i in range(steps):
                    give(a, s, i).wait()

        @pl.when(s >= count)
        def _(s=s):
            for copy in clear(s):
                copy.wait()


def on_device(shard_lost, new_blocks, weights, first_moment, second_moment, gradient):
    _, block, ff = weights.shape
    rows = block // REP
    width = ff + LANES
    f32 = jnp.float32
    vmem, anywhere = pl.BlockSpec(memory_space=pltpu.VMEM), pl.BlockSpec(memory_space=pl.ANY)
    smem = pl.BlockSpec(memory_space=pltpu.SMEM)
    hbm = pl.BlockSpec(memory_space=pltpu.HBM)
    gat, gwin, norm, meta = pl.pallas_call(
        gather_kernel,
        out_shape=(
            jax.ShapeDtypeStruct((3, SLOTS, block, width), jnp.int16),
            jax.ShapeDtypeStruct((SHIFT + 1, block, ff), jnp.bfloat16),
            jax.ShapeDtypeStruct((8, 128), f32),
            jax.ShapeDtypeStruct((8,), jnp.int32),
        ),
        in_specs=[hbm] * 6,
        out_specs=(anywhere, anywhere, vmem, smem),
        scratch_shapes=[
            pltpu.SMEM(shard_lost.shape, jnp.int32),
            pltpu.SMEM(new_blocks.shape, jnp.int32),
            pltpu.VMEM((3, rows, ff), f32),
            pltpu.VMEM((3, rows, ff), f32),
            *[pltpu.VMEM((SHIFT + 1, rows, width), jnp.int16)] * 3,
            pltpu.VMEM((3, SLOTS, rows, width), jnp.int16),
            pltpu.VMEM((block, ff), jnp.bfloat16),
            pltpu.VMEM((4, 8, LANES), f32),
            pltpu.VMEM((8, 8, LANES), f32),
            pltpu.SemaphoreType.DMA((10,)),
            pltpu.SemaphoreType.DMA((72,)),
            pltpu.SemaphoreType.DMA((72,)),
        ],
        compiler_params=pltpu.CompilerParams(
            collective_id=0, has_side_effects=True, vmem_limit_bytes=60 * 2**20
        ),
        name="gather_blocks",
    )(shard_lost, new_blocks, weights[0], first_moment[0], second_moment[0], gradient[0])

    limit = 0.5 * math.sqrt(block * WIDE * ff)
    outs = pl.pallas_call(
        functools.partial(update_kernel, limit),
        out_shape=[jax.ShapeDtypeStruct((SLOTS * block, ff), f32)] * 3,
        in_specs=[smem, vmem, anywhere, anywhere],
        out_specs=[anywhere] * 3,
        scratch_shapes=[
            pltpu.VMEM((3, SLOTS, block, width), jnp.int16),
            pltpu.VMEM((SLOTS, block, ff), jnp.bfloat16),
            pltpu.VMEM((3, SLOTS, block, ff), f32),
            pltpu.VMEM((block, ff), f32),
            pltpu.SemaphoreType.DMA((3, SLOTS)),
            pltpu.SemaphoreType.DMA((SLOTS,)),
            pltpu.SemaphoreType.DMA((3, SLOTS, block // STEP)),
            pltpu.SemaphoreType.DMA((3, SLOTS)),
        ],
        compiler_params=pltpu.CompilerParams(vmem_limit_bytes=60 * 2**20),
        name="adam_update",
    )(meta, norm, gat, gwin)
    return tuple(out[None] for out in outs)


def solution(mesh):
    split = P("rep", "wide", None)
    return jax.shard_map(
        on_device,
        mesh=mesh,
        in_specs=(P(), P(), split, split, split, split),
        out_specs=(split, split, split),
        check_vma=False,
    )
```

```python
import functools
import math

import jax
import jax.numpy as jnp
from jax import lax
from jax.experimental import pallas as pl
from jax.experimental.pallas import tpu as pltpu
from jax.sharding import PartitionSpec as P

beta_first = 0.9
beta_second = 0.95
bias_first = 1.0 - 0.9**20
bias_second = 1.0 - 0.95**20
learn_rate = 0.01
weight_decay = 0.1
eps_adam = 1e-08

WIDE = 32
REP = 8
ROW = 4
SHIFT = 4
SLOTS = 3
LANES = 128
TOP = 32767.0
CHUNKS = 4
STEP = 32
STAGE_TWO = tuple(range(ROW, WIDE, ROW))
MESH = pl.DeviceIdType.MESH


def encode(x, out):
    size = jnp.abs(x)
    most = jnp.clip(jnp.max(size, axis=1, keepdims=True), 2.0**-120, 2.0**120)
    exponent = jnp.ceil(jnp.log2(most))
    code = jnp.minimum(jnp.round(jnp.sqrt(size * jnp.exp2(-exponent)) * TOP), TOP)
    code = jnp.where(x < 0, -code, code)
    out[:, : x.shape[1]] = code.astype(jnp.int32).astype(jnp.int16)
    tail = jnp.broadcast_to(exponent, (x.shape[0], LANES))
    out[:, x.shape[1] :] = tail.astype(jnp.int32).astype(jnp.int16)


def decode(x, times):
    columns = x.shape[1] - LANES
    code = x[:, :columns].astype(jnp.int32).astype(jnp.float32)
    scale = jnp.exp2(x[:, columns:].astype(jnp.int32).astype(jnp.float32)) * (times / TOP**2)
    return code * jnp.abs(code) * jnp.concatenate([scale] * (columns // LANES), axis=1)


def fold(squares):
    top = squares[:8] + squares[8:]
    parts = [top[:, LANES * c : LANES * (c + 1)] for c in range(top.shape[1] // LANES)]
    while len(parts) > 1:
        parts = [sum(parts[i : i + 2][1:], parts[i]) for i in range(0, len(parts), 2)]
    return parts[0]


def gather_kernel(
    lost_hbm, blocks_hbm, w_ref, m_ref, v_ref, g_ref,
    gat_ref, gwin_ref, norm_ref, meta_ref,
    lost_ref, blocks_ref, own, fix, win_w, win_m, win_v, sel, gv, part_one, part_two, loc, out_sem, in_sem,
):
    arrays = (w_ref, m_ref, v_ref)
    wins = (win_w, win_m, win_v)
    rows = own.shape[1]
    island = lax.axis_index("rep")
    shard = lax.axis_index("wide")
    partner = island + 1 - 2 * lax.rem(island, 2)
    width = sel.shape[3]
    middle = width // LANES // 2 * LANES
    left, right = pl.ds(0, middle), pl.ds(middle, width - middle)
    to_partner = {"rep": partner, "wide": shard}
    used = {"remote": 0, "local": 0}

    def lower(d):
        return {"rep": island, "wide": lax.rem(shard + WIDE - d, WIDE)}

    def higher(d):
        return {"rep": island, "wide": lax.rem(shard + d, WIDE)}

    column = lax.rem(shard, ROW)

    def in_row(d):
        return {"rep": island, "wide": shard - column + lax.rem(column + ROW - d, ROW)}

    def along_y(dy):
        return lax.rem(island + REP + 2 * dy, REP)

    def chip_y(dy):
        return {"rep": along_y(dy), "wide": shard}

    def piece(p):
        return pl.ds(pl.multiple_of(p * rows, rows), rows)

    def maker(where):
        k = used["remote"]
        used["remote"] = k + 1

        def make(src, dst):
            return pltpu.make_async_remote_copy(
                src, dst, out_sem.at[k], in_sem.at[k], device_id=where, device_id_type=MESH
            )

        return make

    def local(src, dst):
        k = used["local"]
        used["local"] = k + 1
        copy = pltpu.make_async_copy(src, dst, loc.at[k])
        copy.start()
        return copy

    sent, kept = [], []

    def ship(src, dst, where, lands=None):
        make = maker(where)
        copy = make(src, dst)
        copy.start()
        sent.append(copy)
        return copy if lands is None else make(src, lands)

    def ship_in_row(d, own_src, above_src, dst):
        make = maker(in_row(d))
        copy = make(own_src, dst)
        sent.append(copy)

        @pl.when(column >= d)
        def _():
            copy.start()

        def go():
            @pl.when(column < d)
            def _():
                make(above_src, dst).start()

        return copy, go

    grad_in = local(g_ref, gv)
    own_in = [local(arrays[a].at[piece(island)], own.at[a]) for a in range(3)]
    lost_in, blocks_in = local(lost_hbm, lost_ref), local(blocks_hbm, blocks_ref)

    barrier = pltpu.get_barrier_semaphore()
    offsets = (1, *STAGE_TWO, WIDE - 1)
    greeted = [*(higher(d) for d in offsets), *(in_row(d) for d in range(1, ROW)), chip_y(1), chip_y(-1), to_partner]
    for device in greeted:
        pl.semaphore_signal(barrier, inc=1, device_id=device, device_id_type=MESH)
    pl.semaphore_wait(barrier, len(greeted))

    mend = [ship(arrays[a].at[piece(partner)], fix.at[a], to_partner) for a in range(3)]

    gstep = gv.shape[0] // CHUNKS
    gone = [pl.ds(c * gstep, gstep) for c in range(CHUNKS)]
    grads = {d: [None] * CHUNKS for d in range(1, SHIFT + 1)}
    grad_go = [None] * CHUNKS

    def grad_first(c):
        rows_c = gone[c]
        grads[4][c] = ship(g_ref.at[rows_c], gwin_ref.at[4, rows_c], lower(4))
        grad_go[c] = []
        for d in (1, 3):
            grads[d][c], go = ship_in_row(d, g_ref.at[rows_c], gwin_ref.at[4, rows_c], gwin_ref.at[d, rows_c])
            grad_go[c].append(go)

    def grad_second(c):
        grads[4][c].wait_recv()
        for go in grad_go[c]:
            go()

    def grad_two(c, d):
        grads[d][c].wait_recv()
        to = lower(1) if d == 1 else higher(1)
        grads[2][c] = ship(gwin_ref.at[d, gone[c]], gwin_ref.at[2, gone[c]], to)

    grad_first(0)

    lost_in.wait()
    blocks_in.wait()
    first = jnp.int32(0)
    count = jnp.int32(0)
    for k in range(blocks_ref.shape[0]):
        n = blocks_ref[k]
        first = first + jnp.where(k < shard, n, 0)
        count = count + jnp.where(k == shard, n, 0)
    gaps = [jnp.clip(first + s - shard, 0, SHIFT) for s in range(SLOTS)]
    meta_ref[0] = count
    for s in range(SLOTS):
        meta_ref[1 + s] = gaps[s]
    broken = lost_ref[island] == shard

    windows, ring, far, across = [], [], [], []

    def code(a):
        own_in[a].wait()
        mend[a].wait_recv()
        encode(jnp.where(broken, fix[a], own[a]), wins[a].at[0])

    def first(a):
        win = wins[a]
        down = ship(win.at[0], win.at[4], lower(4))
        windows.append((down, [ship_in_row(d, win.at[0], win.at[4], win.at[d]) for d in (2, 1, 3)]))

    def second(a):
        windows[a][0].wait_recv()
        for _, go in windows[a][1]:
            go()

    def pick(a):
        for lands, _ in windows[a][1]:
            lands.wait_recv()
        for s in range(SLOTS):
            sel[a, s] = wins[a][gaps[s]]
        mine = gat_ref.at[a, :, piece(island)]
        ring.append(
            (
                ship(sel.at[a], mine, chip_y(1), lands=gat_ref.at[a, :, piece(along_y(-1))]),
                ship(sel.at[a], mine, chip_y(-1), lands=gat_ref.at[a, :, piece(along_y(1))]),
            )
        )
        across.append(ship(sel.at[a], mine, to_partner, lands=gat_ref.at[a, :, piece(partner)]))
        kept.append(local(sel.at[a], mine))

    def cross(a, dy):
        theirs = gat_ref.at[a, :, piece(along_y(dy))]
        lands = gat_ref.at[a, :, piece(lax.rem(partner + REP + 2 * dy, REP))]
        across.append(ship(theirs, theirs, to_partner, lands=lands))

    def pass_on(a):
        halves = []
        for copy, dy, half in ((ring[a][0], 1, left), (ring[a][1], -1, right)):
            copy.wait_recv()
            theirs = gat_ref.at[a, :, piece(along_y(-dy)), half]
            halves.append(ship(theirs, theirs, chip_y(dy), lands=gat_ref.at[a, :, piece(along_y(2)), half]))
            cross(a, -dy)
        far.append(halves)

    def close(a):
        for copy in far[a]:
            copy.wait_recv()
        cross(a, 2)

    grad_in.wait()
    kept.append(local(gv, gwin_ref.at[0]))
    step = 16

    def add_rows(i, total):
        x = gv[pl.ds(pl.multiple_of(i * step, step), step), :].astype(jnp.float32)
        return total + fold(x * x)

    part_one[0] = lax.fori_loop(0, gv.shape[0] // step, add_rows, jnp.zeros((8, LANES), jnp.float32))
    ones = [ship(part_one.at[0], part_one.at[d], in_row(d)) for d in range(1, ROW)]

    code(0)
    first(0)
    code(1)
    first(1)
    code(2)
    first(2)
    second(0)
    second(1)
    second(2)
    pick(0)
    grad_second(0)
    pick(1)
    for c in range(1, CHUNKS):
        grad_first(c)
    for copy in ones:
        copy.wait_recv()
    part_two[0] = part_one[0] + part_one[1] + part_one[2] + part_one[3]
    twos = [ship(part_two.at[0], part_two.at[k + 1], lower(d)) for k, d in enumerate(STAGE_TWO)]
    grad_two(0, 3)
    pick(2)
    grad_second(1)
    pass_on(0)
    grad_second(2)
    grad_two(1, 3)
    pass_on(1)
    grad_second(3)
    grad_two(2, 3)
    pass_on(2)
    grad_two(3, 1)
    close(0)
    close(1)
    close(2)

    for copy in twos:
        copy.wait_recv()
    total = part_two[0]
    for k in range(1, len(STAGE_TWO) + 1):
        total = total + part_two[k]
    norm_ref[...] = total

    for copy in (grads[1][0], grads[1][1], grads[1][2], grads[3][3], *grads[2], *across):
        copy.wait_recv()
    for copy in sent:
        copy.wait_send()
    for copy in kept:
        copy.wait()


def update_kernel(
    limit, meta_ref, norm_ref, gat_ref, gwin_ref, w_out, m_out, v_out,
    codes, grads, fresh, zeros, in_sem, grad_sem, out_sem, zero_sem,
):
    outs = (w_out, m_out, v_out)
    block = codes.shape[2]
    steps = block // STEP
    count = meta_ref[0]

    def fetch(s):
        copies = [pltpu.make_async_copy(gat_ref.at[a, s], codes.at[a, s], in_sem.at[a, s]) for a in range(3)]
        return (*copies, pltpu.make_async_copy(gwin_ref.at[meta_ref[1 + s]], grads.at[s], grad_sem.at[s]))

    def clear(s):
        return [pltpu.make_async_copy(zeros, outs[a].at[pl.ds(s * block, block)], zero_sem.at[a, s]) for a in range(3)]

    def give(a, s, i):
        rows = pl.ds(pl.multiple_of(i * STEP, STEP), STEP)
        there = pl.ds(pl.multiple_of(s * block + i * STEP, STEP), STEP)
        return pltpu.make_async_copy(fresh.at[a, s, rows], outs[a].at[there], out_sem.at[a, s, i])

    for s in range(SLOTS):

        @pl.when(s < count)
        def _(s=s):
            for copy in fetch(s):
                copy.start()

    zeros[...] = jnp.zeros_like(zeros)
    for s in range(SLOTS):

        @pl.when(s >= count)
        def _(s=s):
            for copy in clear(s):
                copy.start()

    norm_sum = jnp.sum(norm_ref[...], keepdims=True)
    factor = jnp.minimum(1.0, limit / (jnp.sqrt(norm_sum) + 1e-06))
    share_one = (1.0 - beta_first) * factor
    share_two = (1.0 - beta_second) * factor * factor

    for s in range(SLOTS):

        @pl.when(s < count)
        def _(s=s):
            for copy in fetch(s):
                copy.wait()

            def some_rows(i, carry):
                rows = pl.ds(pl.multiple_of(i * STEP, STEP), STEP)
                grad = grads[s, rows].astype(jnp.float32)
                one_new = decode(codes[1, s, rows], beta_first) + grad * share_one
                two_new = decode(codes[2, s, rows], beta_second) + grad * grad * share_two
                scaled = two_new * (1.0 / bias_second)
                step_dir = one_new * (learn_rate / bias_first) / (scaled * lax.rsqrt(scaled) + eps_adam)
                fresh[0, s, rows] = decode(codes[0, s, rows], 1.0 - learn_rate * weight_decay) - step_dir
                fresh[1, s, rows] = one_new
                fresh[2, s, rows] = two_new
                for a in range(3):
                    give(a, s, i).start()
                return carry

            lax.fori_loop(0, steps, some_rows, 0)

    for s in range(SLOTS):

        @pl.when(s < count)
        def _(s=s):
            for a in range(3):
                for i in range(steps):
                    give(a, s, i).wait()

        @pl.when(s >= count)
        def _(s=s):
            for copy in clear(s):
                copy.wait()


def on_device(shard_lost, new_blocks, weights, first_moment, second_moment, gradient):
    _, block, ff = weights.shape
    rows = block // REP
    width = ff + LANES
    f32 = jnp.float32
    vmem, anywhere = pl.BlockSpec(memory_space=pltpu.VMEM), pl.BlockSpec(memory_space=pl.ANY)
    smem = pl.BlockSpec(memory_space=pltpu.SMEM)
    hbm = pl.BlockSpec(memory_space=pltpu.HBM)
    gat, gwin, norm, meta = pl.pallas_call(
        gather_kernel,
        out_shape=(
            jax.ShapeDtypeStruct((3, SLOTS, block, width), jnp.int16),
            jax.ShapeDtypeStruct((SHIFT + 1, block, ff), jnp.bfloat16),
            jax.ShapeDtypeStruct((8, 128), f32),
            jax.ShapeDtypeStruct((8,), jnp.int32),
        ),
        in_specs=[hbm] * 6,
        out_specs=(anywhere, anywhere, vmem, smem),
        scratch_shapes=[
            pltpu.SMEM(shard_lost.shape, jnp.int32),
            pltpu.SMEM(new_blocks.shape, jnp.int32),
            pltpu.VMEM((3, rows, ff), f32),
            pltpu.VMEM((3, rows, ff), f32),
            *[pltpu.VMEM((SHIFT + 1, rows, width), jnp.int16)] * 3,
            pltpu.VMEM((3, SLOTS, rows, width), jnp.int16),
            pltpu.VMEM((block, ff), jnp.bfloat16),
            pltpu.VMEM((4, 8, LANES), f32),
            pltpu.VMEM((8, 8, LANES), f32),
            pltpu.SemaphoreType.DMA((10,)),
            pltpu.SemaphoreType.DMA((72,)),
            pltpu.SemaphoreType.DMA((72,)),
        ],
        compiler_params=pltpu.CompilerParams(
            collective_id=0, has_side_effects=True, vmem_limit_bytes=60 * 2**20
        ),
        name="gather_blocks",
    )(shard_lost, new_blocks, weights[0], first_moment[0], second_moment[0], gradient[0])

    limit = 0.5 * math.sqrt(block * WIDE * ff)
    outs = pl.pallas_call(
        functools.partial(update_kernel, limit),
        out_shape=[jax.ShapeDtypeStruct((SLOTS * block, ff), f32)] * 3,
        in_specs=[smem, vmem, anywhere, anywhere],
        out_specs=[anywhere] * 3,
        scratch_shapes=[
            pltpu.VMEM((3, SLOTS, block, width), jnp.int16),
            pltpu.VMEM((SLOTS, block, ff), jnp.bfloat16),
            pltpu.VMEM((3, SLOTS, block, ff), f32),
            pltpu.VMEM((block, ff), f32),
            pltpu.SemaphoreType.DMA((3, SLOTS)),
            pltpu.SemaphoreType.DMA((SLOTS,)),
            pltpu.SemaphoreType.DMA((3, SLOTS, block // STEP)),
            pltpu.SemaphoreType.DMA((3, SLOTS)),
        ],
        compiler_params=pltpu.CompilerParams(vmem_limit_bytes=60 * 2**20),
        name="adam_update",
    )(meta, norm, gat, gwin)
    return tuple(out[None] for out in outs)


def solution(mesh):
    split = P("rep", "wide", None)
    return jax.shard_map(
        on_device,
        mesh=mesh,
        in_specs=(P(), P(), split, split, split, split),
        out_specs=(split, split, split),
        check_vma=False,
    )
```

```python
import functools
import math

import jax
import jax.numpy as jnp
from jax import lax
from jax.experimental import pallas as pl
from jax.experimental.pallas import tpu as pltpu
from jax.sharding import PartitionSpec as P

beta_first = 0.9
beta_second = 0.95
bias_first = 1.0 - 0.9**20
bias_second = 1.0 - 0.95**20
learn_rate = 0.01
weight_decay = 0.1
eps_adam = 1e-08

WIDE = 32
REP = 8
ROW = 4
SHIFT = 4
SLOTS = 3
LANES = 128
TOP = 32767.0
CHUNKS = 4
STEP = 32
STAGE_TWO = tuple(range(ROW, WIDE, ROW))
MESH = pl.DeviceIdType.MESH


def lanes_of(width):
    return (width - LANES, width - LANES, width)


def encode(x, out):
    size = jnp.abs(x)
    most = jnp.clip(jnp.max(size, axis=1, keepdims=True), 2.0**-120, 2.0**120)
    exponent = jnp.ceil(jnp.log2(most))
    code = jnp.minimum(jnp.round(jnp.sqrt(size * jnp.exp2(-exponent)) * TOP), TOP)
    out[:, : x.shape[1]] = jnp.where(x < 0, -code, code).astype(jnp.int32).astype(jnp.int16)
    return jnp.broadcast_to(exponent, (x.shape[0], LANES))


def decode(x, scale, times):
    code = x.astype(jnp.int32).astype(jnp.float32)
    scale = jnp.broadcast_to(scale * (times / TOP**2), (x.shape[0], LANES))
    return code * jnp.abs(code) * jnp.concatenate([scale] * (x.shape[1] // LANES), axis=1)


def fold(squares):
    top = squares[:8] + squares[8:]
    parts = [top[:, LANES * c : LANES * (c + 1)] for c in range(top.shape[1] // LANES)]
    while len(parts) > 1:
        parts = [sum(parts[i : i + 2][1:], parts[i]) for i in range(0, len(parts), 2)]
    return parts[0]


def gather_kernel(
    lost_hbm, blocks_hbm, w_ref, m_ref, v_ref, g_ref,
    gat_ref, gwin_ref, norm_ref, meta_ref,
    lost_ref, blocks_ref, own, fix, gv, part_one, part_two, loc, out_sem, in_sem, *buffers,
):
    arrays = (w_ref, m_ref, v_ref)
    units = lanes_of(gat_ref.shape[3])
    wins, sels = buffers[:3], buffers[3:]
    rows = own.shape[1]
    island = lax.axis_index("rep")
    shard = lax.axis_index("wide")
    partner = island + 1 - 2 * lax.rem(island, 2)
    to_partner = {"rep": partner, "wide": shard}
    used = {"remote": 0, "local": 0}

    def lower(d):
        return {"rep": island, "wide": lax.rem(shard + WIDE - d, WIDE)}

    def higher(d):
        return {"rep": island, "wide": lax.rem(shard + d, WIDE)}

    column = lax.rem(shard, ROW)

    def in_row(d):
        return {"rep": island, "wide": shard - column + lax.rem(column + ROW - d, ROW)}

    def along_y(dy):
        return lax.rem(island + REP + 2 * dy, REP)

    def chip_y(dy):
        return {"rep": along_y(dy), "wide": shard}

    def piece(p):
        return pl.ds(pl.multiple_of(p * rows, rows), rows)

    def maker(where):
        k = used["remote"]
        used["remote"] = k + 1

        def make(src, dst):
            return pltpu.make_async_remote_copy(
                src, dst, out_sem.at[k], in_sem.at[k], device_id=where, device_id_type=MESH
            )

        return make

    def local(src, dst):
        k = used["local"]
        used["local"] = k + 1
        copy = pltpu.make_async_copy(src, dst, loc.at[k])
        copy.start()
        return copy

    sent, kept = [], []

    def ship(src, dst, where, lands=None):
        make = maker(where)
        copy = make(src, dst)
        copy.start()
        sent.append(copy)
        return copy if lands is None else make(src, lands)

    def ship_in_row(d, own_src, above_src, dst):
        make = maker(in_row(d))
        copy = make(own_src, dst)
        sent.append(copy)

        @pl.when(column >= d)
        def _():
            copy.start()

        def go():
            @pl.when(column < d)
            def _():
                make(above_src, dst).start()

        return copy, go

    grad_in = local(g_ref, gv)
    own_in = [local(arrays[a].at[piece(island)], own.at[a]) for a in range(3)]
    lost_in, blocks_in = local(lost_hbm, lost_ref), local(blocks_hbm, blocks_ref)

    barrier = pltpu.get_barrier_semaphore()
    offsets = (1, *STAGE_TWO, WIDE - 1)
    greeted = [*(higher(d) for d in offsets), *(in_row(d) for d in range(1, ROW)), chip_y(1), chip_y(-1), to_partner]
    for device in greeted:
        pl.semaphore_signal(barrier, inc=1, device_id=device, device_id_type=MESH)
    pl.semaphore_wait(barrier, len(greeted))

    mend = [ship(arrays[a].at[piece(partner)], fix.at[a], to_partner) for a in range(3)]

    gstep = gv.shape[0] // CHUNKS
    gone = [pl.ds(c * gstep, gstep) for c in range(CHUNKS)]
    grads = {d: [None] * CHUNKS for d in range(1, SHIFT + 1)}
    grad_go = [None] * CHUNKS

    def grad_first(c):
        rows_c = gone[c]
        grads[4][c] = ship(g_ref.at[rows_c], gwin_ref.at[4, rows_c], lower(4))
        grad_go[c] = []
        for d in (1, 3):
            grads[d][c], go = ship_in_row(d, g_ref.at[rows_c], gwin_ref.at[4, rows_c], gwin_ref.at[d, rows_c])
            grad_go[c].append(go)

    def grad_second(c):
        grads[4][c].wait_recv()
        for go in grad_go[c]:
            go()

    def grad_two(c, d):
        grads[d][c].wait_recv()
        to = lower(1) if d == 1 else higher(1)
        grads[2][c] = ship(gwin_ref.at[d, gone[c]], gwin_ref.at[2, gone[c]], to)

    grad_first(0)

    lost_in.wait()
    blocks_in.wait()
    first = jnp.int32(0)
    count = jnp.int32(0)
    for k in range(blocks_ref.shape[0]):
        n = blocks_ref[k]
        first = first + jnp.where(k < shard, n, 0)
        count = count + jnp.where(k == shard, n, 0)
    gaps = [jnp.clip(first + s - shard, 0, SHIFT) for s in range(SLOTS)]
    meta_ref[0] = count
    for s in range(SLOTS):
        meta_ref[1 + s] = gaps[s]
    broken = lost_ref[island] == shard

    windows, ring, far, across = [], [], [], []

    tails = []

    def code(a):
        own_in[a].wait()
        mend[a].wait_recv()
        tails.append(encode(jnp.where(broken, fix[a], own[a]), wins[a].at[0]))
        if a == 2:
            lane = lax.broadcasted_iota(jnp.int32, tails[0].shape, 1)
            tail = jnp.where(lane == 0, tails[0], jnp.where(lane == 1, tails[1], tails[2]))
            wins[2][0, :, units[1] :] = tail.astype(jnp.int32).astype(jnp.int16)

    def first(u):
        win = wins[u]
        down = ship(win.at[0], win.at[4], lower(4))
        windows.append((down, [ship_in_row(d, win.at[0], win.at[4], win.at[d]) for d in (2, 1, 3)]))

    def second(u):
        windows[u][0].wait_recv()
        for _, go in windows[u][1]:
            go()

    def slot(u, p, half=None):
        start, lanes = 0, units[u]
        middle = lanes // LANES // 2 * LANES
        if half is not None:
            start, lanes = (start, middle) if half == 0 else (start + middle, lanes - middle)
        return gat_ref.at[u, :, piece(p), pl.ds(start, lanes)]

    def pick(u):
        for lands, _ in windows[u][1]:
            lands.wait_recv()
        for s in range(SLOTS):
            sels[u][s] = wins[u][gaps[s]]
        mine = slot(u, island)
        ring.append(
            (
                ship(sels[u], mine, chip_y(1), lands=slot(u, along_y(-1))),
                ship(sels[u], mine, chip_y(-1), lands=slot(u, along_y(1))),
            )
        )
        across.append(ship(sels[u], mine, to_partner, lands=slot(u, partner)))
        kept.append(local(sels[u], mine))

    def cross(u, dy):
        theirs = slot(u, along_y(dy))
        across.append(ship(theirs, theirs, to_partner, lands=slot(u, lax.rem(partner + REP + 2 * dy, REP))))

    def pass_on(u):
        halves = []
        for half, dy in enumerate((1, -1)):
            ring[u][half].wait_recv()
            theirs = slot(u, along_y(-dy), half)
            halves.append(ship(theirs, theirs, chip_y(dy), lands=slot(u, along_y(2), half)))
            cross(u, -dy)
        far.append(halves)

    def close(u):
        for copy in far[u]:
            copy.wait_recv()
        cross(u, 2)

    grad_in.wait()
    kept.append(local(gv, gwin_ref.at[0]))
    step = 16

    def add_rows(i, total):
        x = gv[pl.ds(pl.multiple_of(i * step, step), step), :].astype(jnp.float32)
        return total + fold(x * x)

    part_one[0] = lax.fori_loop(0, gv.shape[0] // step, add_rows, jnp.zeros((8, LANES), jnp.float32))
    ones = [ship(part_one.at[0], part_one.at[d], in_row(d)) for d in range(1, ROW)]

    code(0)
    first(0)
    code(1)
    first(1)
    code(2)
    first(2)
    second(0)
    second(1)
    second(2)
    pick(0)
    grad_second(0)
    pick(1)
    for c in range(1, CHUNKS):
        grad_first(c)
    for copy in ones:
        copy.wait_recv()
    part_two[0] = part_one[0] + part_one[1] + part_one[2] + part_one[3]
    twos = [ship(part_two.at[0], part_two.at[k + 1], lower(d)) for k, d in enumerate(STAGE_TWO)]
    grad_two(0, 3)
    pick(2)
    grad_second(1)
    pass_on(0)
    grad_second(2)
    grad_two(1, 3)
    pass_on(1)
    grad_second(3)
    grad_two(2, 3)
    pass_on(2)
    grad_two(3, 1)
    close(0)
    close(1)
    close(2)

    for copy in twos:
        copy.wait_recv()
    total = part_two[0]
    for k in range(1, len(STAGE_TWO) + 1):
        total = total + part_two[k]
    norm_ref[...] = total

    for copy in (grads[1][0], grads[1][1], grads[1][2], grads[3][3], *grads[2], *across):
        copy.wait_recv()
    for copy in sent:
        copy.wait_send()
    for copy in kept:
        copy.wait()


def update_kernel(
    limit, meta_ref, norm_ref, gat_ref, gwin_ref, w_out, m_out, v_out,
    codes, grads, fresh, zeros, in_sem, grad_sem, out_sem, zero_sem,
):
    outs = (w_out, m_out, v_out)
    block = codes.shape[2]
    steps = block // STEP
    count = meta_ref[0]
    columns = fresh.shape[3]

    def fetch(s):
        copies = []
        for a, lanes in enumerate(lanes_of(codes.shape[3])):
            part = pl.ds(0, lanes)
            copies.append(
                pltpu.make_async_copy(gat_ref.at[a, s, :, part], codes.at[a, s, :, part], in_sem.at[a, s])
            )
        return (*copies, pltpu.make_async_copy(gwin_ref.at[meta_ref[1 + s]], grads.at[s], grad_sem.at[s]))

    def clear(s):
        return [pltpu.make_async_copy(zeros, outs[a].at[pl.ds(s * block, block)], zero_sem.at[a, s]) for a in range(3)]

    def give(a, s, i):
        rows = pl.ds(pl.multiple_of(i * STEP, STEP), STEP)
        there = pl.ds(pl.multiple_of(s * block + i * STEP, STEP), STEP)
        return pltpu.make_async_copy(fresh.at[a, s, rows], outs[a].at[there], out_sem.at[a, s, i])

    for s in range(SLOTS):

        @pl.when(s < count)
        def _(s=s):
            for copy in fetch(s):
                copy.start()

    zeros[...] = jnp.zeros_like(zeros)
    for s in range(SLOTS):

        @pl.when(s >= count)
        def _(s=s):
            for copy in clear(s):
                copy.start()

    norm_sum = jnp.sum(norm_ref[...], keepdims=True)
    factor = jnp.minimum(1.0, limit / (jnp.sqrt(norm_sum) + 1e-06))
    share_one = (1.0 - beta_first) * factor
    share_two = (1.0 - beta_second) * factor * factor

    for s in range(SLOTS):

        @pl.when(s < count)
        def _(s=s):
            for copy in fetch(s):
                copy.wait()

            def some_rows(i, carry):
                rows = pl.ds(pl.multiple_of(i * STEP, STEP), STEP)
                grad = grads[s, rows].astype(jnp.float32)
                scale = jnp.exp2(codes[2, s, rows, columns:].astype(jnp.int32).astype(jnp.float32))
                one_new = decode(codes[1, s, rows, :columns], scale[:, 1:2], beta_first) + grad * share_one
                two_new = decode(codes[2, s, rows, :columns], scale[:, 2:3], beta_second) + grad * grad * share_two
                scaled = two_new * (1.0 / bias_second)
                step_dir = one_new * (learn_rate / bias_first) / (scaled * lax.rsqrt(scaled) + eps_adam)
                fresh[0, s, rows] = decode(codes[0, s, rows, :columns], scale[:, 0:1], 1.0 - learn_rate * weight_decay) - step_dir
                fresh[1, s, rows] = one_new
                fresh[2, s, rows] = two_new
                for a in range(3):
                    give(a, s, i).start()
                return carry

            lax.fori_loop(0, steps, some_rows, 0)

    for s in range(SLOTS):

        @pl.when(s < count)
        def _(s=s):
            for a in range(3):
                for i in range(steps):
                    give(a, s, i).wait()

        @pl.when(s >= count)
        def _(s=s):
            for copy in clear(s):
                copy.wait()


def on_device(shard_lost, new_blocks, weights, first_moment, second_moment, gradient):
    _, block, ff = weights.shape
    rows = block // REP
    width = ff + LANES
    f32 = jnp.float32
    vmem, anywhere = pl.BlockSpec(memory_space=pltpu.VMEM), pl.BlockSpec(memory_space=pl.ANY)
    smem = pl.BlockSpec(memory_space=pltpu.SMEM)
    hbm = pl.BlockSpec(memory_space=pltpu.HBM)
    gat, gwin, norm, meta = pl.pallas_call(
        gather_kernel,
        out_shape=(
            jax.ShapeDtypeStruct((3, SLOTS, block, width), jnp.int16),
            jax.ShapeDtypeStruct((SHIFT + 1, block, ff), jnp.bfloat16),
            jax.ShapeDtypeStruct((8, 128), f32),
            jax.ShapeDtypeStruct((8,), jnp.int32),
        ),
        in_specs=[hbm] * 6,
        out_specs=(anywhere, anywhere, vmem, smem),
        scratch_shapes=[
            pltpu.SMEM(shard_lost.shape, jnp.int32),
            pltpu.SMEM(new_blocks.shape, jnp.int32),
            pltpu.VMEM((3, rows, ff), f32),
            pltpu.VMEM((3, rows, ff), f32),
            pltpu.VMEM((block, ff), jnp.bfloat16),
            pltpu.VMEM((4, 8, LANES), f32),
            pltpu.VMEM((8, 8, LANES), f32),
            pltpu.SemaphoreType.DMA((12,)),
            pltpu.SemaphoreType.DMA((104,)),
            pltpu.SemaphoreType.DMA((104,)),
            *[pltpu.VMEM((SHIFT + 1, rows, lanes), jnp.int16) for lanes in lanes_of(width)],
            *[pltpu.VMEM((SLOTS, rows, lanes), jnp.int16) for lanes in lanes_of(width)],
        ],
        compiler_params=pltpu.CompilerParams(
            collective_id=0, has_side_effects=True, vmem_limit_bytes=60 * 2**20
        ),
        name="gather_blocks",
    )(shard_lost, new_blocks, weights[0], first_moment[0], second_moment[0], gradient[0])

    limit = 0.5 * math.sqrt(block * WIDE * ff)
    outs = pl.pallas_call(
        functools.partial(update_kernel, limit),
        out_shape=[jax.ShapeDtypeStruct((SLOTS * block, ff), f32)] * 3,
        in_specs=[smem, vmem, anywhere, anywhere],
        out_specs=[anywhere] * 3,
        scratch_shapes=[
            pltpu.VMEM((3, SLOTS, block, width), jnp.int16),
            pltpu.VMEM((SLOTS, block, ff), jnp.bfloat16),
            pltpu.VMEM((3, SLOTS, block, ff), f32),
            pltpu.VMEM((block, ff), f32),
            pltpu.SemaphoreType.DMA((3, SLOTS)),
            pltpu.SemaphoreType.DMA((SLOTS,)),
            pltpu.SemaphoreType.DMA((3, SLOTS, block // STEP)),
            pltpu.SemaphoreType.DMA((3, SLOTS)),
        ],
        compiler_params=pltpu.CompilerParams(vmem_limit_bytes=60 * 2**20),
        name="adam_update",
    )(meta, norm, gat, gwin)
    return tuple(out[None] for out in outs)


def solution(mesh):
    split = P("rep", "wide", None)
    return jax.shard_map(
        on_device,
        mesh=mesh,
        in_specs=(P(), P(), split, split, split, split),
        out_specs=(split, split, split),
        check_vma=False,
    )
```

```python
import functools
import math

import jax
import jax.numpy as jnp
from jax import lax
from jax.experimental import pallas as pl
from jax.experimental.pallas import tpu as pltpu
from jax.sharding import PartitionSpec as P

beta_first = 0.9
beta_second = 0.95
bias_first = 1.0 - 0.9**20
bias_second = 1.0 - 0.95**20
learn_rate = 0.01
weight_decay = 0.1
eps_adam = 1e-08

WIDE = 32
REP = 8
ROW = 4
SHIFT = 4
SLOTS = 3
LANES = 128
TOP = 32767.0
CHUNKS = 4
STEP = 32
STAGE_TWO = tuple(range(ROW, WIDE, ROW))
MESH = pl.DeviceIdType.MESH


def encode(x, out):
    size = jnp.abs(x)
    most = jnp.clip(jnp.max(size, axis=1, keepdims=True), 2.0**-120, 2.0**120)
    exponent = jnp.ceil(jnp.log2(most))
    code = jnp.minimum(jnp.round(jnp.sqrt(size * jnp.exp2(-exponent)) * TOP), TOP)
    code = jnp.where(x < 0, -code, code)
    out[:, : x.shape[1]] = code.astype(jnp.int32).astype(jnp.int16)
    tail = jnp.broadcast_to(exponent, (x.shape[0], LANES))
    out[:, x.shape[1] :] = tail.astype(jnp.int32).astype(jnp.int16)


def decode(x, scale):
    code = x.astype(jnp.int32).astype(jnp.float32)
    return code * jnp.abs(code) * scale


def fold(squares):
    top = squares[:8] + squares[8:]
    parts = [top[:, LANES * c : LANES * (c + 1)] for c in range(top.shape[1] // LANES)]
    while len(parts) > 1:
        parts = [sum(parts[i : i + 2][1:], parts[i]) for i in range(0, len(parts), 2)]
    return parts[0]


def gather_kernel(
    lost_hbm, blocks_hbm, w_ref, m_ref, v_ref, g_ref,
    gat_ref, gwin_ref, norm_ref, meta_ref,
    lost_ref, blocks_ref, own, fix, win_w, win_m, win_v, sel, gv, part_one, part_two, loc, out_sem, in_sem,
):
    arrays = (w_ref, m_ref, v_ref)
    wins = (win_w, win_m, win_v)
    rows = own.shape[1]
    island = lax.axis_index("rep")
    shard = lax.axis_index("wide")
    partner = island + 1 - 2 * lax.rem(island, 2)
    width = sel.shape[3]
    middle = width // LANES // 2 * LANES
    left, right = pl.ds(0, middle), pl.ds(middle, width - middle)
    to_partner = {"rep": partner, "wide": shard}
    used = {"remote": 0, "local": 0}

    def lower(d):
        return {"rep": island, "wide": lax.rem(shard + WIDE - d, WIDE)}

    def higher(d):
        return {"rep": island, "wide": lax.rem(shard + d, WIDE)}

    column = lax.rem(shard, ROW)

    def in_row(d):
        return {"rep": island, "wide": shard - column + lax.rem(column + ROW - d, ROW)}

    def along_y(dy):
        return lax.rem(island + REP + 2 * dy, REP)

    def chip_y(dy):
        return {"rep": along_y(dy), "wide": shard}

    def piece(p):
        return pl.ds(pl.multiple_of(p * rows, rows), rows)

    def maker(where):
        k = used["remote"]
        used["remote"] = k + 1

        def make(src, dst):
            return pltpu.make_async_remote_copy(
                src, dst, out_sem.at[k], in_sem.at[k], device_id=where, device_id_type=MESH
            )

        return make

    def local(src, dst):
        k = used["local"]
        used["local"] = k + 1
        copy = pltpu.make_async_copy(src, dst, loc.at[k])
        copy.start()
        return copy

    sent, kept = [], []

    def ship(src, dst, where, lands=None):
        make = maker(where)
        copy = make(src, dst)
        copy.start()
        sent.append(copy)
        return copy if lands is None else make(src, lands)

    def ship_in_row(d, own_src, above_src, dst):
        make = maker(in_row(d))
        copy = make(own_src, dst)
        sent.append(copy)

        @pl.when(column >= d)
        def _():
            copy.start()

        def go():
            @pl.when(column < d)
            def _():
                make(above_src, dst).start()

        return copy, go

    grad_in = local(g_ref, gv)
    own_in = [local(arrays[a].at[piece(island)], own.at[a]) for a in range(3)]
    lost_in, blocks_in = local(lost_hbm, lost_ref), local(blocks_hbm, blocks_ref)

    barrier = pltpu.get_barrier_semaphore()
    offsets = (1, *STAGE_TWO, WIDE - 1)
    greeted = [*(higher(d) for d in offsets), *(in_row(d) for d in range(1, ROW)), chip_y(1), chip_y(-1), to_partner]
    for device in greeted:
        pl.semaphore_signal(barrier, inc=1, device_id=device, device_id_type=MESH)
    pl.semaphore_wait(barrier, len(greeted))

    mend = [ship(arrays[a].at[piece(partner)], fix.at[a], to_partner) for a in range(3)]

    gstep = gv.shape[0] // CHUNKS
    gone = [pl.ds(c * gstep, gstep) for c in range(CHUNKS)]
    grads = {d: [None] * CHUNKS for d in range(1, SHIFT + 1)}
    grad_go = [None] * CHUNKS

    def grad_first(c):
        rows_c = gone[c]
        grads[4][c] = ship(g_ref.at[rows_c], gwin_ref.at[4, rows_c], lower(4))
        grad_go[c] = []
        for d in (1, 3):
            grads[d][c], go = ship_in_row(d, g_ref.at[rows_c], gwin_ref.at[4, rows_c], gwin_ref.at[d, rows_c])
            grad_go[c].append(go)

    def grad_second(c):
        grads[4][c].wait_recv()
        for go in grad_go[c]:
            go()

    def grad_two(c, d):
        grads[d][c].wait_recv()
        to = lower(1) if d == 1 else higher(1)
        grads[2][c] = ship(gwin_ref.at[d, gone[c]], gwin_ref.at[2, gone[c]], to)

    grad_first(0)

    lost_in.wait()
    blocks_in.wait()
    first = jnp.int32(0)
    count = jnp.int32(0)
    for k in range(blocks_ref.shape[0]):
        n = blocks_ref[k]
        first = first + jnp.where(k < shard, n, 0)
        count = count + jnp.where(k == shard, n, 0)
    gaps = [jnp.clip(first + s - shard, 0, SHIFT) for s in range(SLOTS)]
    meta_ref[0] = count
    for s in range(SLOTS):
        meta_ref[1 + s] = gaps[s]
    broken = lost_ref[island] == shard

    windows, ring, far, across = [], [], [], []

    def code(a):
        own_in[a].wait()
        mend[a].wait_recv()
        encode(jnp.where(broken, fix[a], own[a]), wins[a].at[0])

    def first(a):
        win = wins[a]
        down = ship(win.at[0], win.at[4], lower(4))
        windows.append((down, [ship_in_row(d, win.at[0], win.at[4], win.at[d]) for d in (2, 1, 3)]))

    def second(a):
        windows[a][0].wait_recv()
        for _, go in windows[a][1]:
            go()

    def pick(a):
        for lands, _ in windows[a][1]:
            lands.wait_recv()
        for s in range(SLOTS):
            sel[a, s] = wins[a][gaps[s]]
        mine = gat_ref.at[a, :, piece(island)]
        ring.append(
            (
                ship(sel.at[a], mine, chip_y(1), lands=gat_ref.at[a, :, piece(along_y(-1))]),
                ship(sel.at[a], mine, chip_y(-1), lands=gat_ref.at[a, :, piece(along_y(1))]),
            )
        )
        across.append(ship(sel.at[a], mine, to_partner, lands=gat_ref.at[a, :, piece(partner)]))
        kept.append(local(sel.at[a], mine))

    def cross(a, dy):
        theirs = gat_ref.at[a, :, piece(along_y(dy))]
        lands = gat_ref.at[a, :, piece(lax.rem(partner + REP + 2 * dy, REP))]
        across.append(ship(theirs, theirs, to_partner, lands=lands))

    def pass_on(a):
        halves = []
        for copy, dy, half in ((ring[a][0], 1, left), (ring[a][1], -1, right)):
            copy.wait_recv()
            theirs = gat_ref.at[a, :, piece(along_y(-dy)), half]
            halves.append(ship(theirs, theirs, chip_y(dy), lands=gat_ref.at[a, :, piece(along_y(2)), half]))
            cross(a, -dy)
        far.append(halves)

    def close(a):
        for copy in far[a]:
            copy.wait_recv()
        cross(a, 2)

    code(0)
    first(0)
    code(1)
    first(1)
    code(2)
    second(0)

    grad_in.wait()
    kept.append(local(gv, gwin_ref.at[0]))
    step = 16

    def add_rows(i, total):
        x = gv[pl.ds(pl.multiple_of(i * step, step), step), :].astype(jnp.float32)
        return total + fold(x * x)

    part_one[0] = lax.fori_loop(0, gv.shape[0] // step, add_rows, jnp.zeros((8, LANES), jnp.float32))
    ones = [ship(part_one.at[0], part_one.at[d], in_row(d)) for d in range(1, ROW)]

    pick(0)
    first(2)
    second(1)
    grad_second(0)
    pick(1)
    second(2)
    for c in range(1, CHUNKS):
        grad_first(c)
    for copy in ones:
        copy.wait_recv()
    part_two[0] = part_one[0] + part_one[1] + part_one[2] + part_one[3]
    twos = [ship(part_two.at[0], part_two.at[k + 1], lower(d)) for k, d in enumerate(STAGE_TWO)]
    grad_two(0, 3)
    pick(2)
    grad_second(1)
    pass_on(0)
    grad_second(2)
    grad_two(1, 3)
    pass_on(1)
    grad_second(3)
    grad_two(2, 3)
    pass_on(2)
    grad_two(3, 1)
    close(0)
    close(1)
    close(2)

    for copy in twos:
        copy.wait_recv()
    total = part_two[0]
    for k in range(1, len(STAGE_TWO) + 1):
        total = total + part_two[k]
    norm_ref[...] = total

    for copy in (grads[1][0], grads[1][1], grads[1][2], grads[3][3], *grads[2], *across):
        copy.wait_recv()
    for copy in sent:
        copy.wait_send()
    for copy in kept:
        copy.wait()


def update_kernel(
    limit, meta_ref, norm_ref, gat_ref, gwin_ref, w_out, m_out, v_out,
    codes, grads, fresh, zeros, in_sem, grad_sem, out_sem, zero_sem,
):
    outs = (w_out, m_out, v_out)
    block = codes.shape[2]
    steps = block // STEP
    count = meta_ref[0]
    columns = fresh.shape[3]

    def fetch(s):
        copies = [pltpu.make_async_copy(gat_ref.at[a, s], codes.at[a, s], in_sem.at[a, s]) for a in range(3)]
        return (*copies, pltpu.make_async_copy(gwin_ref.at[meta_ref[1 + s]], grads.at[s], grad_sem.at[s]))

    def clear(s):
        return [pltpu.make_async_copy(zeros, outs[a].at[pl.ds(s * block, block)], zero_sem.at[a, s]) for a in range(3)]

    def give(a, s, i):
        rows = pl.ds(pl.multiple_of(i * STEP, STEP), STEP)
        there = pl.ds(pl.multiple_of(s * block + i * STEP, STEP), STEP)
        return pltpu.make_async_copy(fresh.at[a, s, rows], outs[a].at[there], out_sem.at[a, s, i])

    for s in range(SLOTS):

        @pl.when(s < count)
        def _(s=s):
            for copy in fetch(s):
                copy.start()

    zeros[...] = jnp.zeros_like(zeros)
    for s in range(SLOTS):

        @pl.when(s >= count)
        def _(s=s):
            for copy in clear(s):
                copy.start()

    norm_sum = jnp.sum(norm_ref[...], keepdims=True)
    factor = jnp.minimum(1.0, limit / (jnp.sqrt(norm_sum) + 1e-06))
    share_one = (1.0 - beta_first) * factor
    share_two = (1.0 - beta_second) * factor * factor

    for s in range(SLOTS):

        @pl.when(s < count)
        def _(s=s):
            for copy in fetch(s):
                copy.wait()

            def some_rows(i, carry):
                rows = pl.ds(pl.multiple_of(i * STEP, STEP), STEP)
                times = (1.0 - learn_rate * weight_decay, beta_first, beta_second)
                scales = [
                    jnp.exp2(codes[a, s, rows, columns:].astype(jnp.int32).astype(jnp.float32)) * (times[a] / TOP**2)
                    for a in range(3)
                ]
                for start in range(0, columns, LANES):
                    part = pl.ds(start, LANES)
                    params, moment_one, moment_two = (decode(codes[a, s, rows, part], scales[a]) for a in range(3))
                    grad = grads[s, rows, part].astype(jnp.float32)
                    one_new = moment_one + grad * share_one
                    two_new = moment_two + grad * grad * share_two
                    scaled = two_new * (1.0 / bias_second)
                    step_dir = one_new * (learn_rate / bias_first) / (scaled * lax.rsqrt(scaled) + eps_adam)
                    fresh[0, s, rows, part] = params - step_dir
                    fresh[1, s, rows, part] = one_new
                    fresh[2, s, rows, part] = two_new
                for a in range(3):
                    give(a, s, i).start()
                return carry

            lax.fori_loop(0, steps, some_rows, 0)

    for s in range(SLOTS):

        @pl.when(s < count)
        def _(s=s):
            for a in range(3):
                for i in range(steps):
                    give(a, s, i).wait()

        @pl.when(s >= count)
        def _(s=s):
            for copy in clear(s):
                copy.wait()


def on_device(shard_lost, new_blocks, weights, first_moment, second_moment, gradient):
    _, block, ff = weights.shape
    rows = block // REP
    width = ff + LANES
    f32 = jnp.float32
    vmem, anywhere = pl.BlockSpec(memory_space=pltpu.VMEM), pl.BlockSpec(memory_space=pl.ANY)
    smem = pl.BlockSpec(memory_space=pltpu.SMEM)
    hbm = pl.BlockSpec(memory_space=pltpu.HBM)
    gat, gwin, norm, meta = pl.pallas_call(
        gather_kernel,
        out_shape=(
            jax.ShapeDtypeStruct((3, SLOTS, block, width), jnp.int16),
            jax.ShapeDtypeStruct((SHIFT + 1, block, ff), jnp.bfloat16),
            jax.ShapeDtypeStruct((8, 128), f32),
            jax.ShapeDtypeStruct((8,), jnp.int32),
        ),
        in_specs=[hbm] * 6,
        out_specs=(anywhere, anywhere, vmem, smem),
        scratch_shapes=[
            pltpu.SMEM(shard_lost.shape, jnp.int32),
            pltpu.SMEM(new_blocks.shape, jnp.int32),
            pltpu.VMEM((3, rows, ff), f32),
            pltpu.VMEM((3, rows, ff), f32),
            *[pltpu.VMEM((SHIFT + 1, rows, width), jnp.int16)] * 3,
            pltpu.VMEM((3, SLOTS, rows, width), jnp.int16),
            pltpu.VMEM((block, ff), jnp.bfloat16),
            pltpu.VMEM((4, 8, LANES), f32),
            pltpu.VMEM((8, 8, LANES), f32),
            pltpu.SemaphoreType.DMA((10,)),
            pltpu.SemaphoreType.DMA((72,)),
            pltpu.SemaphoreType.DMA((72,)),
        ],
        compiler_params=pltpu.CompilerParams(
            collective_id=0, has_side_effects=True, vmem_limit_bytes=60 * 2**20
        ),
        name="gather_blocks",
    )(shard_lost, new_blocks, weights[0], first_moment[0], second_moment[0], gradient[0])

    limit = 0.5 * math.sqrt(block * WIDE * ff)
    outs = pl.pallas_call(
        functools.partial(update_kernel, limit),
        out_shape=[jax.ShapeDtypeStruct((SLOTS * block, ff), f32)] * 3,
        in_specs=[smem, vmem, anywhere, anywhere],
        out_specs=[anywhere] * 3,
        scratch_shapes=[
            pltpu.VMEM((3, SLOTS, block, width), jnp.int16),
            pltpu.VMEM((SLOTS, block, ff), jnp.bfloat16),
            pltpu.VMEM((3, SLOTS, block, ff), f32),
            pltpu.VMEM((block, ff), f32),
            pltpu.SemaphoreType.DMA((3, SLOTS)),
            pltpu.SemaphoreType.DMA((SLOTS,)),
            pltpu.SemaphoreType.DMA((3, SLOTS, block // STEP)),
            pltpu.SemaphoreType.DMA((3, SLOTS)),
        ],
        compiler_params=pltpu.CompilerParams(vmem_limit_bytes=60 * 2**20),
        name="adam_update",
    )(meta, norm, gat, gwin)
    return tuple(out[None] for out in outs)


def solution(mesh):
    split = P("rep", "wide", None)
    return jax.shard_map(
        on_device,
        mesh=mesh,
        in_specs=(P(), P(), split, split, split, split),
        out_specs=(split, split, split),
        check_vma=False,
    )
```
